32 devices in a mesh: slab: 8 (over y, x, core), pencil: 4 (over z).
Axes of the slice: x: 2, y: 2, z: 4, core: 2. Of those that a mesh axis runs over, the one named last changes fastest.
Arguments:
- cotangent: float32 [32, 512, 512], P('slab', 'pencil'), may hold values from -6 to 6
- seg_rows: int32 [32, 4], replicated, may hold values from 1 to 64, 128 in all within a row
- owners: int32 [32, 4], replicated, may hold values from 0 to 31
- offsets: int32 [32, 4], replicated, may hold values from 0 to 64
Outputs:
- rhs_grad: float32 [32, 512, 512], P('slab', 'pencil')
- parent_grad: float32 [32, 128, 128], P(('slab', 'pencil'))
The draws below stay inside these ranges and needn't reach their ends.
Inputs may be any that keep to these rules, and one draw needn't show every extreme that they name: `seg_rows`: each tile's 4 row counts sum to 128; in every tile one segment has exactly 64 rows.
All inputs are finite; a program needn't handle non-finite values.
Results may differ from the reference program's by a relative error of at most 0.00002.
Values sent between devices are 32-bit elements; how exact they have to be, the bound alone decides.
A program may use at most 192 MiB of HBM per device.

```python
import math
import jax
import jax.numpy as jnp
import numpy as np
from jax import lax

NZ = 512
TILE = 128
NSEG = 4
MOSTSEG = 64
NX = 32
NY = 512
PTILES = 32
BT = 32


def with_ends(values, own_key, low, top_value):
    place = [jax.random.randint(jax.random.fold_in(own_key, axis), (), 0, length) for axis, length in enumerate(values.shape)]
    main_axis = values.shape.index(max(values.shape))
    beside = place[:main_axis] + [(place[main_axis] + 1) % values.shape[main_axis]] + place[main_axis + 1:]
    return values.at[tuple(place)].set(low).at[tuple(beside)].set(top_value)


def block_levels(stream_key, shape, pieces, low, high):
    factor_of = 1.0
    for axis_at, parts in pieces:
        draws = jax.random.uniform(jax.random.fold_in(jax.random.fold_in(stream_key, 6), axis_at), (parts,), jnp.float32, low / len(pieces), high / len(pieces))
        factor_of = factor_of * jnp.repeat(jnp.exp(draws), shape[axis_at] // parts).reshape((-1,) + (1,) * (len(shape) - 1 - axis_at))
    return factor_of


def rank_table(number_of, lean):
    portions = [(1 << 20) // math.isqrt(rank ** lean) + 1 for rank in range(1, number_of + 1)]
    scale = 1 + sum(portions) // (1 << 30)
    return np.cumsum(np.array([max(1, weight // scale) for weight in portions]))


def skewed_ids(rng, shape, number_of, skew):
    grid = rank_table(number_of, skew)
    lot = jax.random.randint(jax.random.fold_in(rng, 1), shape, 0, int(grid[number_of - 1]))
    grade = jnp.searchsorted(jnp.asarray(grid, jnp.int32), lot, side="right")
    return jax.random.permutation(jax.random.fold_in(rng, 2), number_of)[grade].astype(jnp.int32)


def split_up(number_of, total, reach, slope):
    loads = [(1 << 20) // math.isqrt(grade ** slope) + 1 for grade in range(2, number_of + 1)]
    spare, counts = total - reach - (number_of - 1), [1] * (number_of - 1)
    while spare > 0:
        movable = [i for i in range(number_of - 1) if counts[i] < reach]
        whole, left = sum([loads[i] for i in movable]), spare
        for i in movable:
            extra = min(reach - counts[i], max(1, left * loads[i] // whole), spare)
            counts[i] = counts[i] + extra
            spare = spare - extra
    return np.array([reach] + counts)


def uneven(key, amount, total, most, lean):
    if amount == 2:
        one = jax.random.randint(key, (), max(1, total - most), min(most, total - 1) + 1)
        return jnp.stack([one, total - one])
    tallies = jnp.asarray(split_up(amount, total, most, lean), jnp.int32)
    twos = (amount - 1) // 2
    source_of, receiver = tallies[1:1 + 2 * twos:2], tallies[2:2 + 2 * twos:2]
    margin = jnp.minimum(source_of - 1, most - receiver)
    shifted = jax.random.randint(jax.random.fold_in(key, 1), (twos,), 0, 1 << 20) % (margin + 1)
    tallies = tallies.at[1:1 + 2 * twos:2].set(source_of - shifted).at[2:2 + 2 * twos:2].set(receiver + shifted)
    return tallies[jax.random.permutation(jax.random.fold_in(key, 2), amount)]


def gaussian(stream_key, shape, spread, limit, cuts=(), held_as=jnp.bfloat16):
    values = jax.random.normal(stream_key, shape, jnp.float32) * spread
    if len(cuts) > 0:
        values = block_levels(stream_key, shape, cuts, -0.22, 0.18) * values
    return jnp.clip(values, min=-limit, max=limit).astype(held_as)


def setup_inputs(seed: int = 0) -> dict:
    arg_keys = jax.random.split(jax.random.key(seed), 5)
    return {
        "cotangent": gaussian(arg_keys[0], (NX, NY, NZ), 1.0, 6.0, ((0, 8), (1, 4)), jnp.float32),
        "seg_rows": jax.vmap(lambda own: uneven(own, NSEG, TILE, MOSTSEG, 2))(jax.random.split(arg_keys[1], BT)).reshape((BT, NSEG)).astype(jnp.int32),
        "owners": with_ends(skewed_ids(arg_keys[2], (BT, NSEG), PTILES, 2), jax.random.fold_in(arg_keys[2], 3), 0, PTILES - 1).astype(jnp.int32),
        "offsets": with_ends(jax.random.randint(arg_keys[3], (BT, NSEG), 0, TILE - MOSTSEG + 1), jax.random.fold_in(arg_keys[3], 1), 0, TILE - MOSTSEG).astype(jnp.int32),
    }


omega_weight = 2.0 / 3.0

def neighbour_sum(padded):
    total = padded[2:, 1:-1, 1:-1] + padded[:-2, 1:-1, 1:-1]
    total = total + padded[1:-1, 2:, 1:-1] + padded[1:-1, :-2, 1:-1]
    total = total + padded[1:-1, 1:-1, 2:] + padded[1:-1, 1:-1, :-2]
    return total

def smoothed(field):
    return (1.0 - omega_weight) * field + omega_weight / 6.0 * neighbour_sum(jnp.pad(field, 1))

def laplace(field, level):
    return (6.0 * field - neighbour_sum(jnp.pad(field, 1))) / 4.0 ** level

def coefficient(level):
    return omega_weight * 4.0 ** level / 6.0

def restrict(field):
    x_cells, y_cells, z_cells = field.shape
    blocks = field.reshape(x_cells // 2, 2, y_cells // 2, 2, z_cells // 2, 2)
    return lax.optimization_barrier(jnp.sum(blocks, axis=(1, 3, 5))) * 0.125

def prolong(field):
    return jnp.repeat(jnp.repeat(jnp.repeat(field, 2, axis=0), 2, axis=1), 2, axis=2)

def relax(state, source, level, count):
    for sweep_number in range(count):
        state = smoothed(state) + coefficient(level) * source
    return state

def source_rows(seg_rows, owners, offsets, tile_size):
    starts = jnp.cumsum(seg_rows, axis=1) - seg_rows
    position = jnp.arange(tile_size, dtype=jnp.int32)[None, None, :]
    inside = (position >= starts[:, :, None]) & (position < (starts + seg_rows)[:, :, None])
    value = owners[:, :, None] * tile_size + offsets[:, :, None] + position - starts[:, :, None]
    return lax.optimization_barrier(jnp.sum(jnp.where(inside, value, 0), axis=1)).astype(jnp.int32)

def vcycle(fine_source):
    state = relax(coefficient(0) * fine_source, fine_source, 0, 2)
    medium_source = restrict(fine_source - laplace(state, 0))
    medium = relax(coefficient(1) * medium_source, medium_source, 1, 2)
    coarse_source = restrict(medium_source - laplace(medium, 1))
    coarse = relax(coefficient(2) * coarse_source, coarse_source, 2, 2)
    medium = relax(medium + prolong(coarse), medium_source, 1, 3)
    return relax(state + prolong(medium), fine_source, 0, 3)

def reference(cotangent, seg_rows, owners, offsets):
    rows_read = source_rows(seg_rows, owners, offsets, TILE).reshape(-1)

    def forward(source, parent):
        picked = parent.reshape(PTILES * TILE, TILE)[rows_read]
        faces = picked.reshape(2, NY // TILE, NZ // TILE, TILE, TILE).transpose(0, 1, 3, 2, 4).reshape(2, NY, NZ)
        total = source.at[0].add(faces[0]).at[NX - 1].add(faces[1])
        return vcycle(total)
    zero_source = jnp.zeros_like(cotangent)
    zero_parent = jnp.zeros((PTILES, TILE, TILE), cotangent.dtype)
    result, pullback = jax.vjp(forward, zero_source, zero_parent)
    rhs_grad, parent_grad = pullback(cotangent)
    return (rhs_grad, parent_grad)
```

```python
import functools
import jax
import jax.numpy as jnp
from jax import lax
from jax.experimental import pallas as pl
from jax.experimental.pallas import tpu as pltpu
from jax.sharding import PartitionSpec as P

TILE = 128
W = 2.0 / 3.0
EDGE = 8
ROUNDS = 14
MESH = pl.DeviceIdType.MESH


def coefficient(level):
    return W * 4.0**level / 6.0


def split3(x):
    hi = x.astype(jnp.bfloat16)
    rest = x - hi.astype(jnp.float32)
    mid = rest.astype(jnp.bfloat16)
    lo = (rest - mid.astype(jnp.float32)).astype(jnp.bfloat16)
    return hi, mid, lo


def times01(x, table):
    hi, mid, lo = split3(x)
    dot = functools.partial(jnp.dot, preferred_element_type=jnp.float32)
    return dot(hi, table) + (dot(mid, table) + dot(lo, table))


def from01(table, x):
    hi, mid, lo = split3(x)
    dot = functools.partial(jnp.dot, preferred_element_type=jnp.float32)
    return dot(table, hi) + (dot(table, mid) + dot(table, lo))


def pair_table(fine, coarse, shift, transposed):
    shape = (fine, coarse) if not transposed else (coarse, fine)
    f = lax.broadcasted_iota(jnp.int32, shape, 1 if transposed else 0)
    c = lax.broadcasted_iota(jnp.int32, shape, 0 if transposed else 1)
    return (((f + shift) // 2) == c).astype(jnp.float32).astype(jnp.bfloat16)


def cycle_kernel(
    S, Q, cot, rhs,
    f0, f1, f2, g3, m0, m1, m2, m3, c0, c1, gc, bm, n0, n1, gm, bf, h0, h1,
    load_sem, send_sem, recv_sem,
):
    s, q = lax.axis_index("slab"), lax.axis_index("pencil")
    has = (s > 0, s < S - 1, q > 0, q < Q - 1)
    peers = (
        (lax.max(s - 1, 0), q), (lax.min(s + 1, S - 1), q),
        (s, lax.max(q - 1, 0)), (s, lax.min(q + 1, Q - 1)),
    )
    NX, NYL, NZL = cot.shape

    load = pltpu.make_async_copy(cot, f0.at[pl.ds(1, NX), pl.ds(EDGE, NYL)], load_sem)
    load.start()

    barrier = pltpu.get_barrier_semaphore()
    for d in range(4):
        @pl.when(has[d])
        def _():
            pl.semaphore_signal(barrier, inc=1, device_id=peers[d], device_id_type=MESH)
    pl.semaphore_wait(barrier, sum(h.astype(jnp.int32) for h in has))

    def sizes(buf):
        return buf.shape[0] - 2, buf.shape[1] - 2 * EDGE, buf.shape[2]

    def regions(buf):
        nx, ny, _ = sizes(buf)
        own_x, own_y = pl.ds(1, nx), pl.ds(EDGE, ny)
        src = (
            buf.at[1, own_y], buf.at[nx, own_y],
            buf.at[own_x, pl.ds(EDGE, EDGE)], buf.at[own_x, pl.ds(ny, EDGE)],
        )
        halo = (
            buf.at[0, own_y], buf.at[nx + 1, own_y],
            buf.at[own_x, pl.ds(0, EDGE)], buf.at[own_x, pl.ds(EDGE + ny, EDGE)],
        )
        return src, halo

    def copy(rnd, buf, d):
        src, halo = regions(buf)
        return pltpu.make_async_remote_copy(
            src_ref=src[d], dst_ref=halo[d ^ 1],
            send_sem=send_sem.at[rnd, d], recv_sem=recv_sem.at[rnd, d ^ 1],
            device_id=peers[d], device_id_type=MESH,
        )

    def start(rnd, buf, d):
        @pl.when(has[d])
        def _():
            copy(rnd, buf, d).start()

    def arrive(rnd, buf, d):
        src, halo = regions(buf)

        @pl.when(has[d])
        def _():
            pltpu.make_async_remote_copy(
                src_ref=src[d ^ 1], dst_ref=halo[d],
                send_sem=send_sem.at[rnd, d], recv_sem=recv_sem.at[rnd, d],
                device_id=peers[d], device_id_type=MESH,
            ).wait_recv()

    sent = []

    def clear(buf):
        _, halo = regions(buf)
        for d in range(4):
            @pl.when(jnp.logical_not(has[d]))
            def _():
                halo[d][...] = jnp.zeros(halo[d].shape, jnp.float32)

    def neighbours(buf, x, r0, rows):
        z = buf.shape[2]
        big = buf[x, pl.ds(r0, rows + 2 * EDGE), :]
        v = big[EDGE:EDGE + rows]
        nb = buf[x - 1, pl.ds(r0 + EDGE, rows), :] + buf[x + 1, pl.ds(r0 + EDGE, rows), :]
        nb = nb + pltpu.roll(big, 1, 0)[EDGE:EDGE + rows]
        nb = nb + pltpu.roll(big, rows + 2 * EDGE - 1, 0)[EDGE:EDGE + rows]
        lane = lax.broadcasted_iota(jnp.int32, (rows, z), 1)
        nb = nb + jnp.where(lane == 0, 0.0, pltpu.roll(v, 1, 1))
        nb = nb + jnp.where(lane == z - 1, 0.0, pltpu.roll(v, z - 1, 1))
        return v, nb

    def rows_of(buf):
        return min(32, sizes(buf)[1])

    def plane_op(buf, x_first, x_count, body):
        ny, rows = sizes(buf)[1], rows_of(buf)
        per = ny // rows

        def step(i, _):
            x = x_first + i // per
            r0 = pl.multiple_of((i % per) * rows, rows)
            body(x, r0, rows)
            return 0
        lax.fori_loop(0, x_count * per, step, 0)

    def sweep(rnd, buf, finish, out=None, between=None):
        nx = sizes(buf)[0]

        def body(x, r0, rows):
            v, nb = neighbours(buf, x, r0, rows)
            finish(x, r0, rows, v, nb)
        if out is not None:
            clear(out)
        if between is not None:
            between()
        arrive(rnd, buf, 2)
        arrive(rnd, buf, 3)
        if nx > 2:
            plane_op(buf, 2, nx - 2, body)
        arrive(rnd, buf, 0)
        if nx == 1:
            arrive(rnd, buf, 1)
        plane_op(buf, 1, 1, body)
        if out is not None:
            start(rnd + 1, out, 0)
            if nx == 1:
                start(rnd + 1, out, 1)
        if nx > 1:
            arrive(rnd, buf, 1)
            plane_op(buf, nx, 1, body)
            if out is not None:
                start(rnd + 1, out, 1)
        if out is not None:
            start(rnd + 1, out, 2)
            start(rnd + 1, out, 3)
            sent.append((rnd + 1, out))

    def put(out, x, r0, rows, value):
        out[x, pl.ds(r0 + EDGE, rows), :] = value

    def own(buf, x, r0, rows):
        return buf[x, pl.ds(r0 + EDGE, rows), :]

    def smooth_to(out, padded=True):
        def finish(x, r0, rows, v, nb):
            value = (1.0 - W) * v + (W / 6.0) * nb
            if padded:
                put(out, x, r0, rows, value)
            else:
                out[x - 1, pl.ds(r0, rows), :] = value
        return finish

    def restrict(src, dst):
        x, y, z = src.shape
        sz = pair_table(z, z // 2, 0, False)
        sy = pair_table(y, y // 2, 0, True)
        for j in range(x // 2):
            both = src[2 * j] + src[2 * j + 1]
            half = times01(both, sz)
            dst[1 + j, pl.ds(EDGE, y // 2), :] = from01(sy, half)

    def prolong(src, dst):
        nx, ny, z = sizes(src)
        pz = pair_table(2 * z, z, 0, True)
        py = pair_table(2 * ny + 2 * EDGE, ny + 2 * EDGE, EDGE, False)
        pc = pair_table(2 * ny, ny, 0, False)
        for j in range(nx + 2):
            if j == 0 or j == nx + 1:
                wide = times01(src[j, pl.ds(EDGE, ny), :], pz)
                dst[0 if j == 0 else 2 * nx + 1, pl.ds(EDGE, 2 * ny), :] = 0.125 * from01(pc, wide)
            else:
                wide = times01(src[j], pz)
                value = 0.125 * from01(py, wide)
                dst[2 * j - 1] = value
                dst[2 * j] = value

    def send_all(rnd, buf):
        for d in range(4):
            start(rnd, buf, d)
        sent.append((rnd, buf))

    def arrive_all(rnd, buf):
        for d in range(4):
            arrive(rnd, buf, d)

    clear(f0)
    load.wait()
    send_all(0, f0)
    sweep(0, f0, smooth_to(f1), f1)
    sweep(1, f1, smooth_to(f2), f2)
    sweep(2, f2, smooth_to(g3, False))
    clear(m0)
    restrict(g3, m0)
    send_all(3, m0)
    sweep(3, m0, smooth_to(m1), m1)
    sweep(4, m1, smooth_to(m2), m2)
    sweep(5, m2, smooth_to(m3, False))
    clear(c0)
    restrict(m3, c0)
    send_all(6, c0)
    sweep(6, c0, smooth_to(c1), c1)

    def coarse_total(x, r0, rows, v, nb):
        value = (1.0 - W) * v + (W / 6.0) * nb
        put(gc, x, r0, rows, coefficient(2) * (own(c0, x, r0, rows) + own(c1, x, r0, rows) + value))
    sweep(7, c1, coarse_total, gc)
    arrive_all(8, gc)
    prolong(gc, bm)

    def medium_correct(x, r0, rows):
        v, nb = neighbours(bm, x, r0, rows)
        put(n0, x, r0, rows, m3[x - 1, pl.ds(r0, rows), :] - (6.0 * v - nb) * 0.25)
    clear(n0)
    plane_op(n0, 1, sizes(n0)[0], medium_correct)
    send_all(9, n0)
    sweep(9, n0, smooth_to(n1), n1)

    def medium_total(x, r0, rows, v, nb):
        value = (1.0 - W) * v + (W / 6.0) * nb
        total = own(m0, x, r0, rows) + own(m1, x, r0, rows) + own(m2, x, r0, rows)
        total = total + own(n0, x, r0, rows) + v + value
        put(gm, x, r0, rows, coefficient(1) * total + own(bm, x, r0, rows))
    sweep(10, n1, medium_total, gm)
    arrive_all(11, gm)
    prolong(gm, bf)

    def fine_correct(x, r0, rows):
        v, nb = neighbours(bf, x, r0, rows)
        put(h0, x, r0, rows, g3[x - 1, pl.ds(r0, rows), :] - (6.0 * v - nb))
    clear(h0)
    nx = sizes(h0)[0]
    plane_op(h0, 1, 1, fine_correct)
    start(12, h0, 0)
    plane_op(h0, nx, 1, fine_correct)
    start(12, h0, 1)
    plane_op(h0, 2, nx - 2, fine_correct)
    start(12, h0, 2)
    start(12, h0, 3)
    sent.append((12, h0))

    def gather_first():
        def body(x, r0, rows):
            total = own(f0, x, r0, rows) + own(f1, x, r0, rows) + own(f2, x, r0, rows)
            total = total + own(h0, x, r0, rows)
            rhs[x - 1, pl.ds(r0, rows), :] = coefficient(0) * total + own(bf, x, r0, rows)
        plane_op(h0, 1, nx, body)
    sweep(12, h0, smooth_to(h1), h1, between=gather_first)

    def fine_total(x, r0, rows, v, nb):
        value = (1.0 - W) * v + (W / 6.0) * nb
        before = rhs[x - 1, pl.ds(r0, rows), :]
        rhs[x - 1, pl.ds(r0, rows), :] = before + coefficient(0) * (v + value)
    sweep(13, h1, fine_total)
    for rnd, buf in sent:
        for d in range(4):
            @pl.when(has[d])
            def _():
                copy(rnd, buf, d).wait_send()


def run_cycle(cotangent):
    S, Q = lax.axis_size("slab"), lax.axis_size("pencil")
    x, y, z = cotangent.shape

    def padded(level):
        k = 2**level
        return pltpu.VMEM((x // k + 2, y // k + 2 * EDGE, z // k), jnp.float32)

    def plain(level):
        k = 2**level
        return pltpu.VMEM((x // k, y // k, z // k), jnp.float32)
    scratch = [padded(0)] * 3 + [plain(0)] + [padded(1)] * 3 + [plain(1)]
    scratch += [padded(2)] * 3 + [padded(1)] * 4 + [padded(0)] * 3
    scratch += [
        pltpu.SemaphoreType.DMA,
        pltpu.SemaphoreType.DMA((ROUNDS, 4)),
        pltpu.SemaphoreType.DMA((ROUNDS, 4)),
    ]
    return pl.pallas_call(
        functools.partial(cycle_kernel, S, Q),
        out_shape=jax.ShapeDtypeStruct(cotangent.shape, jnp.float32),
        in_specs=[pl.BlockSpec(memory_space=pl.ANY)],
        out_specs=pl.BlockSpec(memory_space=pltpu.VMEM),
        scratch_shapes=scratch,
        compiler_params=pltpu.CompilerParams(
            collective_id=0, has_side_effects=True, vmem_limit_bytes=48 * 2**20
        ),
        name="vcycle",
    )(cotangent)


def source_rows(seg_rows, owners, offsets, tile_size):
    starts = jnp.cumsum(seg_rows, axis=1) - seg_rows
    position = jnp.arange(tile_size, dtype=jnp.int32)[None, None, :]
    inside = (position >= starts[:, :, None]) & (position < (starts + seg_rows)[:, :, None])
    value = owners[:, :, None] * tile_size + offsets[:, :, None] + position - starts[:, :, None]
    return jnp.sum(jnp.where(inside, value, 0), axis=1)


def tile_rows(faces, tile_size):
    face_count, y_cells, z_cells = faces.shape
    blocks = faces.reshape(
        face_count, y_cells // tile_size, tile_size, z_cells // tile_size, tile_size
    )
    return blocks.transpose(0, 1, 3, 2, 4).reshape(-1, tile_size)


def shards(cotangent, seg_rows, owners, offsets):
    rhs_grad = run_cycle(cotangent)
    x_cells = rhs_grad.shape[0]
    slab_index, slab_count = lax.axis_index("slab"), lax.axis_size("slab")
    low_part = jnp.where(slab_index == 0, rhs_grad[0], 0.0)
    high_part = jnp.where(slab_index == slab_count - 1, rhs_grad[x_cells - 1], 0.0)
    summed_faces = lax.psum(jnp.stack([low_part, high_part]), "slab")
    all_faces = lax.all_gather(summed_faces, "pencil", axis=1, tiled=True)
    all_rows = tile_rows(all_faces, TILE)
    targets = source_rows(seg_rows, owners, offsets, TILE).reshape(-1)
    first_row = lax.axis_index(("slab", "pencil")) * TILE
    hot = (targets[None, :] - first_row) == jnp.arange(TILE, dtype=jnp.int32)[:, None]
    owned = jnp.dot(hot.astype(jnp.float32), all_rows, precision=lax.Precision.HIGHEST)
    return (rhs_grad, owned.reshape(1, TILE, TILE))


def solution(mesh):
    return jax.shard_map(
        shards,
        mesh=mesh,
        in_specs=(P("slab", "pencil", None), P(), P(), P()),
        out_specs=(P("slab", "pencil", None), P(("slab", "pencil"), None, None)),
        check_vma=False,
    )
```

```python
import functools
import jax
import jax.numpy as jnp
from jax import lax
from jax.experimental import pallas as pl
from jax.experimental.pallas import tpu as pltpu
from jax.sharding import PartitionSpec as P

TILE = 128
W = 2.0 / 3.0
EDGE = 8
ROUNDS = 14
CHUNKS = 4
MESH = pl.DeviceIdType.MESH


def coefficient(level):
    return W * 4.0**level / 6.0


def split3(x):
    hi = x.astype(jnp.bfloat16)
    rest = x - hi.astype(jnp.float32)
    mid = rest.astype(jnp.bfloat16)
    lo = (rest - mid.astype(jnp.float32)).astype(jnp.bfloat16)
    return hi, mid, lo


def times01(x, table):
    hi, mid, lo = split3(x)
    dot = functools.partial(jnp.dot, preferred_element_type=jnp.float32)
    return dot(hi, table) + (dot(mid, table) + dot(lo, table))


def from01(table, x):
    hi, mid, lo = split3(x)
    dot = functools.partial(jnp.dot, preferred_element_type=jnp.float32)
    return dot(table, hi) + (dot(table, mid) + dot(table, lo))


def pair_table(fine, coarse, shift, transposed):
    shape = (fine, coarse) if not transposed else (coarse, fine)
    f = lax.broadcasted_iota(jnp.int32, shape, 1 if transposed else 0)
    c = lax.broadcasted_iota(jnp.int32, shape, 0 if transposed else 1)
    return (((f + shift) // 2) == c).astype(jnp.float32).astype(jnp.bfloat16)


def face_return(
    s, q, S, Q, pieces, goal, rhs, parent, fa, rows_buf, part_out, part_in,
    piece_send, piece_recv, ring_send, ring_recv, part_send, part_recv,
):
    NX, NYL, NZL = rhs.shape
    R = NYL // pieces
    tiles_z = NZL // TILE
    holders = ((0, 0, 0), (1, S - 1, NX - 1))

    def piece(face, plane, k):
        return pltpu.make_async_remote_copy(
            src_ref=rhs.at[plane, pl.ds(k * R, R)], dst_ref=fa.at[face, q],
            send_sem=piece_send.at[face, k], recv_sem=piece_recv.at[face],
            device_id=(k, q), device_id_type=MESH,
        )
    for face, slab, plane in holders:
        @pl.when(s == slab)
        def _():
            for k in range(pieces):
                if k != slab:
                    piece(face, plane, k).start()
            if slab < pieces:
                fa[face, q] = rhs[plane, pl.ds(slab * R, R), :]

    def ring(k):
        return pltpu.make_async_remote_copy(
            src_ref=fa.at[:, q], dst_ref=fa.at[:, q],
            send_sem=ring_send.at[k], recv_sem=ring_recv.at[k],
            device_id=(s, lax.rem(q + k, Q)), device_id_type=MESH,
        )

    def ring_arrival(k):
        source = lax.rem(q + Q - k, Q)
        return pltpu.make_async_remote_copy(
            src_ref=fa.at[:, source], dst_ref=fa.at[:, source],
            send_sem=ring_send.at[k], recv_sem=ring_recv.at[k],
            device_id=(s, source), device_id_type=MESH,
        )

    def part(k):
        return pltpu.make_async_remote_copy(
            src_ref=part_out.at[k], dst_ref=part_in.at[k],
            send_sem=part_send.at[k], recv_sem=part_recv.at[k],
            device_id=(lax.rem(s + k, S), q), device_id_type=MESH,
        )

    @pl.when(s < pieces)
    def _():
        for face, slab, plane in holders:
            @pl.when(s != slab)
            def _():
                pltpu.make_async_remote_copy(
                    src_ref=fa.at[face, q], dst_ref=fa.at[face, q],
                    send_sem=piece_send.at[face, 0], recv_sem=piece_recv.at[face],
                    device_id=(slab, q), device_id_type=MESH,
                ).wait_recv()
        for k in range(1, Q):
            ring(k).start()
        for k in range(1, Q):
            ring_arrival(k).wait_recv()
        for face in range(2):
            for a in range(Q):
                for b in range(tiles_z):
                    t = (face * Q + a) * tiles_z + b
                    rows_buf[pl.ds(t * R, R), :] = fa[face, a, :, pl.ds(b * TILE, TILE)]
        hi, mid, lo = split3(rows_buf[...])
        dot = functools.partial(jnp.dot, preferred_element_type=jnp.float32)
        count = rows_buf.shape[0]
        local = lax.broadcasted_iota(jnp.int32, (TILE, count), 0)
        for k in list(range(1, S)) + [0]:
            owner = lax.rem(s + k, S) * Q + q
            shifted = goal[...] - owner * TILE
            hot = (shifted == local).astype(jnp.float32).astype(jnp.bfloat16)
            part_out[k] = dot(hot, hi) + (dot(hot, mid) + dot(hot, lo))
            if k > 0:
                part(k).start()

    total = None
    if pieces == S:
        total = part_out[0]
        for k in range(1, S):
            part(k).wait_recv()
            total = total + part_in[k]
        parent[0] = total
    else:
        parent[...] = jnp.zeros_like(parent)

        @pl.when(s < pieces)
        def _():
            parent[0] = part_out[0]
        for k in range(1, S):
            @pl.when(lax.rem(s + S - k, S) < pieces)
            def _():
                part(k).wait_recv()
                parent[0] += part_in[k]

    for face, slab, plane in holders:
        @pl.when(s == slab)
        def _():
            for k in range(pieces):
                if k != slab:
                    piece(face, plane, k).wait_send()

    @pl.when(s < pieces)
    def _():
        for k in range(1, Q):
            ring(k).wait_send()
        for k in range(1, S):
            part(k).wait_send()


def cycle_kernel(
    S, Q, pieces, cot, goal, rhs, parent,
    f0, f1, f2, g3, m0, m1, m2, m3, c0, c1, gc, bm, n0, n1, gm, bf, h0, h1,
    fa, rows_buf, part_out, part_in,
    load_sem, send_sem, recv_sem, piece_send, piece_recv, ring_send, ring_recv, part_send, part_recv,
):
    s, q = lax.axis_index("slab"), lax.axis_index("pencil")
    has = (s > 0, s < S - 1, q > 0, q < Q - 1)
    peers = (
        (lax.max(s - 1, 0), q), (lax.min(s + 1, S - 1), q),
        (s, lax.max(q - 1, 0)), (s, lax.min(q + 1, Q - 1)),
    )
    NX, NYL, NZL = cot.shape

    load = pltpu.make_async_copy(cot, f0.at[pl.ds(1, NX), pl.ds(EDGE, NYL)], load_sem)
    load.start()

    barrier = pltpu.get_barrier_semaphore()
    for k in range(1, S):
        pl.semaphore_signal(
            barrier, inc=1, device_id=(lax.rem(s + k, S), q), device_id_type=MESH)
    for k in range(1, Q):
        pl.semaphore_signal(
            barrier, inc=1, device_id=(s, lax.rem(q + k, Q)), device_id_type=MESH)
    pl.semaphore_wait(barrier, S + Q - 2)

    def sizes(buf):
        return buf.shape[0] - 2, buf.shape[1] - 2 * EDGE, buf.shape[2]

    def chunks(buf, d):
        nx, ny, _ = sizes(buf)
        return CHUNKS if d < 2 and nx > 2 else 1

    def regions(buf, c=0, n=1):
        nx, ny, _ = sizes(buf)
        own_x, own_y = pl.ds(1, nx), pl.ds(EDGE + c * (ny // n), ny // n)
        src = (
            buf.at[1, own_y], buf.at[nx, own_y],
            buf.at[own_x, pl.ds(EDGE, EDGE)], buf.at[own_x, pl.ds(ny, EDGE)],
        )
        halo = (
            buf.at[0, own_y], buf.at[nx + 1, own_y],
            buf.at[own_x, pl.ds(0, EDGE)], buf.at[own_x, pl.ds(EDGE + ny, EDGE)],
        )
        return src, halo

    def copy(rnd, buf, d, c):
        src, halo = regions(buf, c, chunks(buf, d))
        return pltpu.make_async_remote_copy(
            src_ref=src[d], dst_ref=halo[d ^ 1],
            send_sem=send_sem.at[rnd, d, c], recv_sem=recv_sem.at[rnd, d ^ 1, c],
            device_id=peers[d], device_id_type=MESH,
        )

    def start(rnd, buf, d, c=None):
        @pl.when(has[d])
        def _():
            for i in range(chunks(buf, d)) if c is None else (c,):
                copy(rnd, buf, d, i).start()

    def arrive(rnd, buf, d, c=None):
        n = chunks(buf, d)

        @pl.when(has[d])
        def _():
            for i in range(n) if c is None else (c,):
                src, halo = regions(buf, i, n)
                pltpu.make_async_remote_copy(
                    src_ref=src[d ^ 1], dst_ref=halo[d],
                    send_sem=send_sem.at[rnd, d, i], recv_sem=recv_sem.at[rnd, d, i],
                    device_id=peers[d], device_id_type=MESH,
                ).wait_recv()

    sent = []

    def clear(buf):
        _, halo = regions(buf)
        for d in range(4):
            @pl.when(jnp.logical_not(has[d]))
            def _():
                halo[d][...] = jnp.zeros(halo[d].shape, jnp.float32)

    def neighbours(buf, x, r0, rows):
        z = buf.shape[2]
        big = buf[x, pl.ds(r0, rows + 2 * EDGE), :]
        v = big[EDGE:EDGE + rows]
        nb = buf[x - 1, pl.ds(r0 + EDGE, rows), :] + buf[x + 1, pl.ds(r0 + EDGE, rows), :]
        nb = nb + pltpu.roll(big, 1, 0)[EDGE:EDGE + rows]
        nb = nb + pltpu.roll(big, rows + 2 * EDGE - 1, 0)[EDGE:EDGE + rows]
        lane = lax.broadcasted_iota(jnp.int32, (rows, z), 1)
        nb = nb + jnp.where(lane == 0, 0.0, pltpu.roll(v, 1, 1))
        nb = nb + jnp.where(lane == z - 1, 0.0, pltpu.roll(v, z - 1, 1))
        return v, nb

    def rows_of(buf):
        return min(32, sizes(buf)[1])

    def plane_op(buf, x_first, x_count, body):
        ny, rows = sizes(buf)[1], rows_of(buf)
        per = ny // rows

        def step(i, _):
            x = x_first + i // per
            r0 = pl.multiple_of((i % per) * rows, rows)
            body(x, r0, rows)
            return 0
        lax.fori_loop(0, x_count * per, step, 0)

    def sweep(rnd, buf, finish, out=None, between=None):
        nx = sizes(buf)[0]

        def body(x, r0, rows):
            v, nb = neighbours(buf, x, r0, rows)
            finish(x, r0, rows, v, nb)
        if out is not None:
            clear(out)
        if between is not None:
            between()
        arrive(rnd, buf, 2)
        arrive(rnd, buf, 3)
        if nx > 2:
            plane_op(buf, 2, nx - 2, body)
            rows = sizes(buf)[1] // CHUNKS
            for c in range(CHUNKS):
                for d, x in ((0, 1), (1, nx)):
                    arrive(rnd, buf, d, c)
                    body(x, c * rows, rows)
                    if out is not None:
                        start(rnd + 1, out, d, c)
        elif nx == 2:
            for d in range(2):
                arrive(rnd, buf, d)
                plane_op(buf, 1 + d, 1, body)
                if out is not None:
                    start(rnd + 1, out, d)
        else:
            arrive(rnd, buf, 0)
            arrive(rnd, buf, 1)
            plane_op(buf, 1, 1, body)
            if out is not None:
                start(rnd + 1, out, 0)
                start(rnd + 1, out, 1)
        if out is not None:
            start(rnd + 1, out, 2)
            start(rnd + 1, out, 3)
            sent.append((rnd + 1, out))

    def put(out, x, r0, rows, value):
        out[x, pl.ds(r0 + EDGE, rows), :] = value

    def own(buf, x, r0, rows):
        return buf[x, pl.ds(r0 + EDGE, rows), :]

    def smooth_to(out, padded=True):
        def finish(x, r0, rows, v, nb):
            value = (1.0 - W) * v + (W / 6.0) * nb
            if padded:
                put(out, x, r0, rows, value)
            else:
                out[x - 1, pl.ds(r0, rows), :] = value
        return finish

    def restrict(src, dst):
        x, y, z = src.shape
        sz = pair_table(z, z // 2, 0, False)
        sy = pair_table(y, y // 2, 0, True)
        for j in range(x // 2):
            both = src[2 * j] + src[2 * j + 1]
            half = times01(both, sz)
            dst[1 + j, pl.ds(EDGE, y // 2), :] = from01(sy, half)

    def prolong(src, dst):
        nx, ny, z = sizes(src)
        pz = pair_table(2 * z, z, 0, True)
        py = pair_table(2 * ny + 2 * EDGE, ny + 2 * EDGE, EDGE, False)
        pc = pair_table(2 * ny, ny, 0, False)
        for j in range(nx + 2):
            if j == 0 or j == nx + 1:
                wide = times01(src[j, pl.ds(EDGE, ny), :], pz)
                dst[0 if j == 0 else 2 * nx + 1, pl.ds(EDGE, 2 * ny), :] = 0.125 * from01(pc, wide)
            else:
                wide = times01(src[j], pz)
                value = 0.125 * from01(py, wide)
                dst[2 * j - 1] = value
                dst[2 * j] = value

    def send_all(rnd, buf):
        for d in range(4):
            start(rnd, buf, d)
        sent.append((rnd, buf))

    def arrive_all(rnd, buf):
        for d in range(4):
            arrive(rnd, buf, d)

    clear(f0)
    load.wait()
    send_all(0, f0)
    sweep(0, f0, smooth_to(f1), f1)
    sweep(1, f1, smooth_to(f2), f2)
    sweep(2, f2, smooth_to(g3, False))
    clear(m0)
    restrict(g3, m0)
    send_all(3, m0)
    sweep(3, m0, smooth_to(m1), m1)
    sweep(4, m1, smooth_to(m2), m2)
    sweep(5, m2, smooth_to(m3, False))
    clear(c0)
    restrict(m3, c0)
    send_all(6, c0)
    sweep(6, c0, smooth_to(c1), c1)

    def coarse_total(x, r0, rows, v, nb):
        value = (1.0 - W) * v + (W / 6.0) * nb
        put(gc, x, r0, rows, coefficient(2) * (own(c0, x, r0, rows) + own(c1, x, r0, rows) + value))
    sweep(7, c1, coarse_total, gc)
    arrive_all(8, gc)
    prolong(gc, bm)

    def medium_correct(x, r0, rows):
        v, nb = neighbours(bm, x, r0, rows)
        put(n0, x, r0, rows, m3[x - 1, pl.ds(r0, rows), :] - (6.0 * v - nb) * 0.25)
    clear(n0)
    plane_op(n0, 1, sizes(n0)[0], medium_correct)
    send_all(9, n0)
    sweep(9, n0, smooth_to(n1), n1)

    def medium_total(x, r0, rows, v, nb):
        value = (1.0 - W) * v + (W / 6.0) * nb
        total = own(m0, x, r0, rows) + own(m1, x, r0, rows) + own(m2, x, r0, rows)
        total = total + own(n0, x, r0, rows) + v + value
        put(gm, x, r0, rows, coefficient(1) * total + own(bm, x, r0, rows))
    sweep(10, n1, medium_total, gm)
    arrive_all(11, gm)
    prolong(gm, bf)

    def fine_correct(x, r0, rows):
        v, nb = neighbours(bf, x, r0, rows)
        put(h0, x, r0, rows, g3[x - 1, pl.ds(r0, rows), :] - (6.0 * v - nb))
    clear(h0)
    nx = sizes(h0)[0]
    plane_op(h0, 1, 1, fine_correct)
    start(12, h0, 0)
    plane_op(h0, nx, 1, fine_correct)
    start(12, h0, 1)
    plane_op(h0, 2, nx - 2, fine_correct)
    start(12, h0, 2)
    start(12, h0, 3)
    sent.append((12, h0))

    def gather_first():
        def body(x, r0, rows):
            total = own(f0, x, r0, rows) + own(f1, x, r0, rows) + own(f2, x, r0, rows)
            total = total + own(h0, x, r0, rows)
            rhs[x - 1, pl.ds(r0, rows), :] = coefficient(0) * total + own(bf, x, r0, rows)
        plane_op(h0, 1, nx, body)
    sweep(12, h0, smooth_to(h1), h1, between=gather_first)

    def fine_total(x, r0, rows, v, nb):
        value = (1.0 - W) * v + (W / 6.0) * nb
        before = rhs[x - 1, pl.ds(r0, rows), :]
        rhs[x - 1, pl.ds(r0, rows), :] = before + coefficient(0) * (v + value)
    sweep(13, h1, fine_total)
    face_return(
        s, q, S, Q, pieces, goal, rhs, parent, fa, rows_buf, part_out, part_in,
        piece_send, piece_recv, ring_send, ring_recv, part_send, part_recv)
    for rnd, buf in sent:
        for d in range(4):
            @pl.when(has[d])
            def _():
                for c in range(chunks(buf, d)):
                    copy(rnd, buf, d, c).wait_send()


def run_cycle(cotangent, seg_rows, owners, offsets):
    S, Q = lax.axis_size("slab"), lax.axis_size("pencil")
    x, y, z = cotangent.shape
    pieces = min(S, y // EDGE)
    R = y // pieces
    targets = source_rows(seg_rows, owners, offsets, TILE)
    first = jnp.minimum(lax.axis_index("slab"), pieces - 1) * R
    goal = lax.dynamic_slice_in_dim(targets, first, R, axis=1).reshape(1, -1)

    def padded(level):
        k = 2**level
        return pltpu.VMEM((x // k + 2, y // k + 2 * EDGE, z // k), jnp.float32)

    def plain(level):
        k = 2**level
        return pltpu.VMEM((x // k, y // k, z // k), jnp.float32)
    scratch = [padded(0)] * 3 + [plain(0)] + [padded(1)] * 3 + [plain(1)]
    scratch += [padded(2)] * 3 + [padded(1)] * 4 + [padded(0)] * 3
    scratch += [
        pltpu.VMEM((2, Q, R, z), jnp.float32),
        pltpu.VMEM((goal.shape[1], TILE), jnp.float32),
        pltpu.VMEM((S, TILE, TILE), jnp.float32),
        pltpu.VMEM((S, TILE, TILE), jnp.float32),
        pltpu.SemaphoreType.DMA,
        pltpu.SemaphoreType.DMA((ROUNDS, 4, CHUNKS)),
        pltpu.SemaphoreType.DMA((ROUNDS, 4, CHUNKS)),
        pltpu.SemaphoreType.DMA((2, pieces)),
        pltpu.SemaphoreType.DMA((2,)),
        pltpu.SemaphoreType.DMA((Q,)),
        pltpu.SemaphoreType.DMA((Q,)),
        pltpu.SemaphoreType.DMA((S,)),
        pltpu.SemaphoreType.DMA((S,)),
    ]
    return pl.pallas_call(
        functools.partial(cycle_kernel, S, Q, pieces),
        out_shape=(
            jax.ShapeDtypeStruct(cotangent.shape, jnp.float32),
            jax.ShapeDtypeStruct((1, TILE, TILE), jnp.float32),
        ),
        in_specs=[pl.BlockSpec(memory_space=pl.ANY), pl.BlockSpec(memory_space=pltpu.VMEM)],
        out_specs=(pl.BlockSpec(memory_space=pltpu.VMEM), pl.BlockSpec(memory_space=pltpu.VMEM)),
        scratch_shapes=scratch,
        compiler_params=pltpu.CompilerParams(
            collective_id=0, has_side_effects=True, vmem_limit_bytes=48 * 2**20
        ),
        name="vcycle",
    )(cotangent, goal)


def source_rows(seg_rows, owners, offsets, tile_size):
    starts = jnp.cumsum(seg_rows, axis=1) - seg_rows
    position = jnp.arange(tile_size, dtype=jnp.int32)[None, None, :]
    inside = (position >= starts[:, :, None]) & (position < (starts + seg_rows)[:, :, None])
    value = owners[:, :, None] * tile_size + offsets[:, :, None] + position - starts[:, :, None]
    return jnp.sum(jnp.where(inside, value, 0), axis=1)


def shards(cotangent, seg_rows, owners, offsets):
    rhs_grad, parent_grad = run_cycle(cotangent, seg_rows, owners, offsets)
    return (rhs_grad, parent_grad)


def solution(mesh):
    return jax.shard_map(
        shards,
        mesh=mesh,
        in_specs=(P("slab", "pencil", None), P(), P(), P()),
        out_specs=(P("slab", "pencil", None), P(("slab", "pencil"), None, None)),
        check_vma=False,
    )
```

```python
import functools
import jax
import jax.numpy as jnp
from jax import lax
from jax.experimental import pallas as pl
from jax.experimental.pallas import tpu as pltpu
from jax.sharding import PartitionSpec as P

TILE = 128
W = 2.0 / 3.0
EDGE = 8
ROUNDS = 14
CHUNKS = 4
MESH = pl.DeviceIdType.MESH


def coefficient(level):
    return W * 4.0**level / 6.0


def split3(x):
    hi = x.astype(jnp.bfloat16)
    rest = x - hi.astype(jnp.float32)
    mid = rest.astype(jnp.bfloat16)
    lo = (rest - mid.astype(jnp.float32)).astype(jnp.bfloat16)
    return hi, mid, lo


def dot(x, y):
    return jnp.dot(x, y, preferred_element_type=jnp.float32)


def pair_table(fine, coarse, shift, transposed):
    shape = (fine, coarse) if not transposed else (coarse, fine)
    f = lax.broadcasted_iota(jnp.int32, shape, 1 if transposed else 0)
    c = lax.broadcasted_iota(jnp.int32, shape, 0 if transposed else 1)
    return (((f + shift) // 2) == c).astype(jnp.float32).astype(jnp.bfloat16)


def face_steps(
    s, q, S, Q, pieces, goal, rhs, parent, fa, rows_buf, part_out, part_in,
    hot_buf, piece_send, piece_recv, ring_send, ring_recv, part_send, part_recv,
):
    NX, NYL, NZL = rhs.shape
    R = NYL // pieces
    tiles_z = NZL // TILE
    holders = ((0, 0, 0), (1, S - 1, NX - 1))

    def piece(face, plane, k):
        return pltpu.make_async_remote_copy(
            src_ref=rhs.at[plane, pl.ds(k * R, R)], dst_ref=fa.at[face, q],
            send_sem=piece_send.at[face, k], recv_sem=piece_recv.at[face],
            device_id=(k, q), device_id_type=MESH,
        )
    def scatter(d):
        face, slab, plane = holders[d]
        for k in range(pieces):
            if k != slab:
                piece(face, plane, k).start()
        if slab < pieces:
            fa[face, q] = rhs[plane, pl.ds(slab * R, R), :]

    def tables():
        local = lax.broadcasted_iota(jnp.int32, (TILE, goal.shape[1]), 0)
        for k in range(S):
            owner = lax.rem(s + k, S) * Q + q
            hot = (goal[...] - owner * TILE) == local
            hot_buf[pl.ds(k * TILE, TILE), :] = hot.astype(jnp.float32).astype(jnp.bfloat16)

    def ring(k):
        return pltpu.make_async_remote_copy(
            src_ref=fa.at[:, q], dst_ref=fa.at[:, q],
            send_sem=ring_send.at[k], recv_sem=ring_recv.at[k],
            device_id=(s, lax.rem(q + k, Q)), device_id_type=MESH,
        )

    def ring_arrival(k):
        source = lax.rem(q + Q - k, Q)
        return pltpu.make_async_remote_copy(
            src_ref=fa.at[:, source], dst_ref=fa.at[:, source],
            send_sem=ring_send.at[k], recv_sem=ring_recv.at[k],
            device_id=(s, source), device_id_type=MESH,
        )

    def part(k):
        return pltpu.make_async_remote_copy(
            src_ref=part_out.at[k], dst_ref=part_in.at[k],
            send_sem=part_send.at[k], recv_sem=part_recv.at[k],
            device_id=(lax.rem(s + k, S), q), device_id_type=MESH,
        )

    def gather():
        @pl.when(s < pieces)
        def _():
            for face, slab, plane in holders:
                @pl.when(s != slab)
                def _():
                    pltpu.make_async_remote_copy(
                        src_ref=fa.at[face, q], dst_ref=fa.at[face, q],
                        send_sem=piece_send.at[face, 0], recv_sem=piece_recv.at[face],
                        device_id=(slab, q), device_id_type=MESH,
                    ).wait_recv()
            for k in range(1, Q):
                ring(k).start()

    def finish():
        @pl.when(s < pieces)
        def _():
            for k in range(1, Q):
                ring_arrival(k).wait_recv()
            for face in range(2):
                for a in range(Q):
                    for b in range(tiles_z):
                        t = (face * Q + a) * tiles_z + b
                        rows_buf[pl.ds(t * R, R), :] = fa[face, a, :, pl.ds(b * TILE, TILE)]
            parts = jnp.concatenate(split3(rows_buf[...]), axis=1)
            group = 4 if S % 4 == 0 else S
            for g in reversed(range(S // group)):
                sums = dot(hot_buf[pl.ds(g * group * TILE, group * TILE), :], parts)
                sums = sums[:, :TILE] + (sums[:, TILE:2 * TILE] + sums[:, 2 * TILE:])
                for k in range(g * group, (g + 1) * group):
                    part_out[k] = sums[(k - g * group) * TILE:(k - g * group + 1) * TILE]
                    if k > 0:
                        part(k).start()

        total = None
        if pieces == S:
            total = part_out[0]
            for k in range(1, S):
                part(k).wait_recv()
                total = total + part_in[k]
            parent[0] = total
        else:
            parent[...] = jnp.zeros_like(parent)

            @pl.when(s < pieces)
            def _():
                parent[0] = part_out[0]
            for k in range(1, S):
                @pl.when(lax.rem(s + S - k, S) < pieces)
                def _():
                    part(k).wait_recv()
                    parent[0] += part_in[k]

        for face, slab, plane in holders:
            @pl.when(s == slab)
            def _():
                for k in range(pieces):
                    if k != slab:
                        piece(face, plane, k).wait_send()

        @pl.when(s < pieces)
        def _():
            for k in range(1, Q):
                ring(k).wait_send()
            for k in range(1, S):
                part(k).wait_send()

    return scatter, tables, gather, finish


def cycle_kernel(
    S, Q, pieces, cot, goal, rhs, parent,
    f0, f1, f2, g3, m0, m1, m2, m3, c0, c1, gc, bm, n0, n1, gm, bf, h0, h1,
    fa, rows_buf, part_out, part_in, hot_buf,
    load_sem, send_sem, recv_sem, piece_send, piece_recv, ring_send, ring_recv, part_send, part_recv,
):
    s, q = lax.axis_index("slab"), lax.axis_index("pencil")
    has = [s > 0, s < S - 1, q > 0, q < Q - 1]
    corners = ((0, 2), (1, 3), (0, 3), (1, 2))
    has += [jnp.logical_and(has[i], has[j]) for i, j in corners]
    side_s, side_q = (lax.max(s - 1, 0), lax.min(s + 1, S - 1)), (lax.max(q - 1, 0), lax.min(q + 1, Q - 1))
    peers = [(side_s[0], q), (side_s[1], q), (s, side_q[0]), (s, side_q[1])]
    peers += [(side_s[i], side_q[j - 2]) for i, j in corners]
    NX, NYL, NZL = cot.shape
    scatter, tables, gather, finish_faces = face_steps(
        s, q, S, Q, pieces, goal, rhs, parent, fa, rows_buf, part_out, part_in,
        hot_buf, piece_send, piece_recv, ring_send, ring_recv, part_send, part_recv)

    load = pltpu.make_async_copy(cot, f0.at[pl.ds(1, NX), pl.ds(EDGE, NYL)], load_sem)
    load.start()

    barrier = pltpu.get_barrier_semaphore()
    for k in range(1, S):
        pl.semaphore_signal(
            barrier, inc=1, device_id=(lax.rem(s + k, S), q), device_id_type=MESH)
    for k in range(1, Q):
        pl.semaphore_signal(
            barrier, inc=1, device_id=(s, lax.rem(q + k, Q)), device_id_type=MESH)
    for d in range(4, 8):
        @pl.when(has[d])
        def _():
            pl.semaphore_signal(barrier, inc=1, device_id=peers[d], device_id_type=MESH)
    pl.semaphore_wait(barrier, S + Q - 2 + sum(h.astype(jnp.int32) for h in has[4:]))

    def sizes(buf):
        return buf.shape[0] - 2, buf.shape[1] - 2 * EDGE, buf.shape[2]

    def wide(buf):
        return buf is gc or buf is gm

    def sides(buf):
        return range(8) if wide(buf) else range(4)

    def chunks(buf, d):
        return CHUNKS if d < 2 and sizes(buf)[0] > 2 else 1

    def regions(buf, c=0, n=1):
        nx, ny, _ = sizes(buf)
        own_x, own_y = pl.ds(1, nx), pl.ds(EDGE + c * (ny // n), ny // n)
        k = EDGE if wide(buf) else 1
        src_x, halo_x = (1, nx), (0, nx + 1)
        src_y = (pl.ds(EDGE, k), pl.ds(EDGE + ny - k, k))
        halo_y = (pl.ds(EDGE - k, k), pl.ds(EDGE + ny, k))
        src = [buf.at[1, own_y], buf.at[nx, own_y], buf.at[own_x, src_y[0]], buf.at[own_x, src_y[1]]]
        halo = [buf.at[0, own_y], buf.at[nx + 1, own_y], buf.at[own_x, halo_y[0]], buf.at[own_x, halo_y[1]]]
        if wide(buf):
            src += [buf.at[src_x[i], src_y[j - 2]] for i, j in corners]
            halo += [buf.at[halo_x[i], halo_y[j - 2]] for i, j in corners]
        return src, halo

    def copy(rnd, buf, d, c):
        src, halo = regions(buf, c, chunks(buf, d))
        return pltpu.make_async_remote_copy(
            src_ref=src[d], dst_ref=halo[d ^ 1],
            send_sem=send_sem.at[rnd, d, c], recv_sem=recv_sem.at[rnd, d ^ 1, c],
            device_id=peers[d], device_id_type=MESH,
        )

    sent = {}

    def start(rnd, buf, d, c=None):
        sent[rnd] = buf

        @pl.when(has[d])
        def _():
            for i in range(chunks(buf, d)) if c is None else (c,):
                copy(rnd, buf, d, i).start()

    def arrive(rnd, buf, d, c=None):
        n = chunks(buf, d)

        @pl.when(has[d])
        def _():
            for i in range(n) if c is None else (c,):
                src, halo = regions(buf, i, n)
                pltpu.make_async_remote_copy(
                    src_ref=src[d ^ 1], dst_ref=halo[d],
                    send_sem=send_sem.at[rnd, d, i], recv_sem=recv_sem.at[rnd, d, i],
                    device_id=peers[d], device_id_type=MESH,
                ).wait_recv()

    def clear(buf):
        _, halo = regions(buf)
        for d in sides(buf):
            @pl.when(jnp.logical_not(has[d]))
            def _():
                halo[d][...] = jnp.zeros(halo[d].shape, jnp.float32)

    def neighbours(buf, x, r0, rows, before=EDGE, after=EDGE):
        z = buf.shape[2]
        first = r0 + EDGE - before
        count = before + rows + after
        big = buf[x, pl.ds(first, count), :]
        v = big[before:before + rows]
        nb = buf[x - 1, pl.ds(first + before, rows), :] + buf[x + 1, pl.ds(first + before, rows), :]
        nb = nb + pltpu.roll(big, 1, 0)[before:before + rows]
        nb = nb + pltpu.roll(big, count - 1, 0)[before:before + rows]
        lane = lax.broadcasted_iota(jnp.int32, (rows, z), 1)
        nb = nb + jnp.where(lane == 0, 0.0, pltpu.roll(v, 1, 1))
        nb = nb + jnp.where(lane == z - 1, 0.0, pltpu.roll(v, z - 1, 1))
        return v, nb

    def plane_op(buf, x_first, x_count, body):
        ny = sizes(buf)[1]
        rows = min(32, ny)
        per = ny // rows

        def step(i, _):
            body(x_first + i // per, pl.multiple_of((i % per) * rows, rows), rows)
            return 0
        lax.fori_loop(0, x_count * per, step, 0)

    def sweep(rnd, buf, finish, out_rnd=None, out=None, edge_first=None, between=None):
        nx, ny, _ = sizes(buf)

        def body(x, r0, rows):
            v, nb = neighbours(buf, x, r0, rows)
            finish(x, r0, rows, v, nb)

        def wait(d, c=None):
            if rnd is not None:
                arrive(rnd, buf, d, c)

        def send(d, c=None):
            if out is not None:
                start(out_rnd, out, d, c)
        if out is not None:
            clear(out)
        wait(2)
        wait(3)
        if edge_first is not None:
            for d, x in ((0, 1), (1, nx)):
                @pl.when(jnp.logical_not(has[d]))
                def _():
                    plane_op(buf, x, 1, body)
                    edge_first(d)
        if nx > 2 and rnd is not None:
            plane_op(buf, 2, nx - 2, body)
        if between is not None:
            between()
        if nx > 2:
            rows = ny // CHUNKS
            for c in range(CHUNKS):
                for d, x in ((0, 1), (1, nx)):
                    if edge_first is not None:
                        @pl.when(has[d])
                        def _():
                            wait(d, c)
                            body(x, c * rows, rows)
                    else:
                        wait(d, c)
                        body(x, c * rows, rows)
                    send(d, c)
            if rnd is None:
                plane_op(buf, 2, nx - 2, body)
        elif nx == 2:
            for d in range(2):
                wait(d)
                plane_op(buf, 1 + d, 1, body)
                send(d)
        else:
            wait(0)
            wait(1)
            plane_op(buf, 1, 1, body)
            send(0)
            send(1)
        if out is not None:
            for d in sides(out):
                if d >= 2:
                    send(d)

    def put(out, x, r0, rows, value):
        out[x, pl.ds(r0 + EDGE, rows), :] = value

    def own(buf, x, r0, rows):
        return buf[x, pl.ds(r0 + EDGE, rows), :]

    def smooth_to(out):
        def finish(x, r0, rows, v, nb):
            put(out, x, r0, rows, (1.0 - W) * v + (W / 6.0) * nb)
        return finish

    def restrict(src, dst):
        x, y, z = sizes(src)
        clear(dst)
        parts = []
        for j in range(x // 2):
            parts += split3(own(src, 2 * j + 1, 0, y) + own(src, 2 * j + 2, 0, y))
        half = dot(jnp.concatenate(parts, axis=0), pair_table(z, z // 2, 0, False))
        sy = pair_table(y, y // 2, 0, True)
        for j in range(x // 2):
            both = half[3 * j * y:(3 * j + 1) * y]
            both = both + (half[(3 * j + 1) * y:(3 * j + 2) * y] + half[(3 * j + 2) * y:(3 * j + 3) * y])
            hi, mid, lo = split3(both)
            put(dst, 1 + j, 0, y // 2, dot(sy, hi) + (dot(sy, mid) + dot(sy, lo)))

    def prolong(src, dst):
        nx, ny, z = sizes(src)
        py = pair_table(2 * ny + 2 * EDGE, ny + 2 * EDGE, EDGE, False)
        pz = pair_table(2 * z, z, 0, True)
        for j in range(nx + 2):
            tall = [dot(py, part).astype(jnp.bfloat16) for part in split3(src[j])]
            n = tall[0].shape[0]
            both = dot(jnp.concatenate(tall, axis=0), pz)
            value = 0.125 * (both[:n] + (both[n:2 * n] + both[2 * n:]))
            dst[2 * j] = value
            dst[2 * j + 1] = value

    def correct(back, old, out, scale):
        nx, ny, _ = sizes(out)

        def body(x, r0, rows, before=EDGE, after=EDGE):
            v, nb = neighbours(back, x + 1, r0, rows, before, after)
            put(out, x, r0, rows, own(old, x, r0, rows) - scale * (6.0 * v - nb))
        clear(out)
        plane_op(out, 1, nx, body)
        for d, x in ((0, 0), (1, nx + 1)):
            @pl.when(has[d])
            def _():
                plane_op(out, x, 1, body)
        for d, r0, before, after in ((2, -EDGE, 0, EDGE), (3, ny, EDGE, 0)):
            @pl.when(has[d])
            def _():
                for x in range(1, nx + 1):
                    body(x, r0, EDGE, before, after)

    def send_all(rnd, buf):
        for d in sides(buf):
            start(rnd, buf, d)

    def arrive_all(rnd, buf):
        for d in sides(buf):
            arrive(rnd, buf, d)

    def send_early(c):
        start(12, g3, 0, c)
        start(12, g3, 1, c)

    clear(f0)
    load.wait()
    send_all(0, f0)
    tables()
    sweep(0, f0, smooth_to(f1), 1, f1)
    sweep(1, f1, smooth_to(f2), 2, f2)
    sweep(2, f2, smooth_to(g3))
    restrict(g3, m0)
    send_all(3, m0)
    send_early(0)
    start(12, g3, 2)
    start(12, g3, 3)
    sweep(3, m0, smooth_to(m1), 4, m1)
    send_early(1)
    sweep(4, m1, smooth_to(m2), 5, m2)
    send_early(2)
    sweep(5, m2, smooth_to(m3))
    restrict(m3, c0)
    send_all(6, c0)
    send_all(9, m3)
    sweep(6, c0, smooth_to(c1), 7, c1)
    send_early(3)

    def coarse_total(x, r0, rows, v, nb):
        value = (1.0 - W) * v + (W / 6.0) * nb
        put(gc, x, r0, rows, coefficient(2) * (own(c0, x, r0, rows) + own(c1, x, r0, rows) + value))
    sweep(7, c1, coarse_total, 8, gc)
    arrive_all(8, gc)
    prolong(gc, bm)
    arrive_all(9, m3)
    correct(bm, m3, n0, 0.25)
    sweep(None, n0, smooth_to(n1), 10, n1)

    def medium_total(x, r0, rows, v, nb):
        value = (1.0 - W) * v + (W / 6.0) * nb
        total = own(m0, x, r0, rows) + own(m1, x, r0, rows) + own(m2, x, r0, rows)
        total = total + own(n0, x, r0, rows) + v + value
        put(gm, x, r0, rows, coefficient(1) * total + own(bm, x + 1, r0, rows))
    sweep(10, n1, medium_total, 11, gm)
    arrive_all(11, gm)
    prolong(gm, bf)
    arrive_all(12, g3)
    correct(bf, g3, h0, 1.0)
    sweep(None, h0, smooth_to(h1), 13, h1)

    def first_terms(x, r0, rows):
        total = own(f0, x, r0, rows) + own(f1, x, r0, rows) + own(f2, x, r0, rows)
        total = total + own(h0, x, r0, rows)
        rhs[x - 1, pl.ds(r0, rows), :] = coefficient(0) * total + own(bf, x + 1, r0, rows)
    plane_op(h0, 1, NX, first_terms)

    def last_terms(x, r0, rows, v, nb):
        value = (1.0 - W) * v + (W / 6.0) * nb
        before = rhs[x - 1, pl.ds(r0, rows), :]
        rhs[x - 1, pl.ds(r0, rows), :] = before + coefficient(0) * (v + value)
    sweep(13, h1, last_terms, edge_first=scatter, between=gather)
    finish_faces()
    for rnd, buf in sent.items():
        for d in sides(buf):
            @pl.when(has[d])
            def _():
                for c in range(chunks(buf, d)):
                    copy(rnd, buf, d, c).wait_send()


def run_cycle(cotangent, seg_rows, owners, offsets):
    S, Q = lax.axis_size("slab"), lax.axis_size("pencil")
    x, y, z = cotangent.shape
    pieces = min(S, y // EDGE)
    R = y // pieces
    targets = source_rows(seg_rows, owners, offsets, TILE)
    first = jnp.minimum(lax.axis_index("slab"), pieces - 1) * R
    goal = lax.dynamic_slice_in_dim(targets, first, R, axis=1).reshape(1, -1)

    def padded(level, deep=1):
        k = 2**level
        return pltpu.VMEM((x // k + 2 * deep, y // k + 2 * EDGE, z // k), jnp.float32)
    scratch = [padded(0)] * 4 + [padded(1)] * 4 + [padded(2)] * 3
    scratch += [padded(1, 2)] + [padded(1)] * 3 + [padded(0, 2)] + [padded(0)] * 2
    scratch += [
        pltpu.VMEM((2, Q, R, z), jnp.float32),
        pltpu.VMEM((goal.shape[1], TILE), jnp.float32),
        pltpu.VMEM((S, TILE, TILE), jnp.float32),
        pltpu.VMEM((S, TILE, TILE), jnp.float32),
        pltpu.VMEM((S * TILE, goal.shape[1]), jnp.bfloat16),
        pltpu.SemaphoreType.DMA,
        pltpu.SemaphoreType.DMA((ROUNDS, 8, CHUNKS)),
        pltpu.SemaphoreType.DMA((ROUNDS, 8, CHUNKS)),
        pltpu.SemaphoreType.DMA((2, pieces)),
        pltpu.SemaphoreType.DMA((2,)),
        pltpu.SemaphoreType.DMA((Q,)),
        pltpu.SemaphoreType.DMA((Q,)),
        pltpu.SemaphoreType.DMA((S,)),
        pltpu.SemaphoreType.DMA((S,)),
    ]
    return pl.pallas_call(
        functools.partial(cycle_kernel, S, Q, pieces),
        out_shape=(
            jax.ShapeDtypeStruct(cotangent.shape, jnp.float32),
            jax.ShapeDtypeStruct((1, TILE, TILE), jnp.float32),
        ),
        in_specs=[pl.BlockSpec(memory_space=pl.ANY), pl.BlockSpec(memory_space=pltpu.VMEM)],
        out_specs=(pl.BlockSpec(memory_space=pltpu.VMEM), pl.BlockSpec(memory_space=pltpu.VMEM)),
        scratch_shapes=scratch,
        compiler_params=pltpu.CompilerParams(
            collective_id=0, has_side_effects=True, vmem_limit_bytes=48 * 2**20
        ),
        name="vcycle",
    )(cotangent, goal)


def source_rows(seg_rows, owners, offsets, tile_size):
    starts = jnp.cumsum(seg_rows, axis=1) - seg_rows
    position = jnp.arange(tile_size, dtype=jnp.int32)[None, None, :]
    inside = (position >= starts[:, :, None]) & (position < (starts + seg_rows)[:, :, None])
    value = owners[:, :, None] * tile_size + offsets[:, :, None] + position - starts[:, :, None]
    return jnp.sum(jnp.where(inside, value, 0), axis=1)


def shards(cotangent, seg_rows, owners, offsets):
    rhs_grad, parent_grad = run_cycle(cotangent, seg_rows, owners, offsets)
    return (rhs_grad, parent_grad)


def solution(mesh):
    return jax.shard_map(
        shards,
        mesh=mesh,
        in_specs=(P("slab", "pencil", None), P(), P(), P()),
        out_specs=(P("slab", "pencil", None), P(("slab", "pencil"), None, None)),
        check_vma=False,
    )
```

```python
import functools
import jax
import jax.numpy as jnp
from jax import lax
from jax.experimental import pallas as pl
from jax.experimental.pallas import tpu as pltpu
from jax.sharding import PartitionSpec as P

TILE = 128
W = 2.0 / 3.0
EDGE = 8
ROUNDS = 14
CHUNKS = 4
MESH = pl.DeviceIdType.MESH


def coefficient(level):
    return W * 4.0**level / 6.0


def split3(x):
    hi = x.astype(jnp.bfloat16)
    rest = x - hi.astype(jnp.float32)
    mid = rest.astype(jnp.bfloat16)
    lo = (rest - mid.astype(jnp.float32)).astype(jnp.bfloat16)
    return hi, mid, lo


def dot(x, y):
    return jnp.dot(x, y, preferred_element_type=jnp.float32)


def pair_table(fine, coarse, shift, transposed):
    shape = (fine, coarse) if not transposed else (coarse, fine)
    f = lax.broadcasted_iota(jnp.int32, shape, 1 if transposed else 0)
    c = lax.broadcasted_iota(jnp.int32, shape, 0 if transposed else 1)
    return (((f + shift) // 2) == c).astype(jnp.float32).astype(jnp.bfloat16)


def face_steps(
    s, q, S, Q, pieces, goal, rhs, parent, fa, rows_buf, part_out, part_in,
    hot_buf, piece_send, piece_recv, ring_send, ring_recv, part_send, part_recv,
):
    NX, NYL, NZL = rhs.shape
    R = NYL // pieces
    tiles_z = NZL // TILE
    holders = ((0, 0, 0), (1, S - 1, NX - 1))

    def piece(face, plane, k):
        return pltpu.make_async_remote_copy(
            src_ref=rhs.at[plane, pl.ds(k * R, R)], dst_ref=fa.at[face, q],
            send_sem=piece_send.at[face, k], recv_sem=piece_recv.at[face],
            device_id=(k, q), device_id_type=MESH,
        )
    def scatter(d):
        face, slab, plane = holders[d]
        for k in range(pieces):
            if k != slab:
                piece(face, plane, k).start()
        if slab < pieces:
            fa[face, q] = rhs[plane, pl.ds(slab * R, R), :]

    def tables():
        local = lax.broadcasted_iota(jnp.int32, (TILE, goal.shape[1]), 0)
        for k in range(S):
            owner = lax.rem(s + k, S) * Q + q
            hot = (goal[...] - owner * TILE) == local
            hot_buf[pl.ds(k * TILE, TILE), :] = hot.astype(jnp.float32).astype(jnp.bfloat16)

    def ring(k):
        return pltpu.make_async_remote_copy(
            src_ref=fa.at[:, q], dst_ref=fa.at[:, q],
            send_sem=ring_send.at[k], recv_sem=ring_recv.at[k],
            device_id=(s, lax.rem(q + k, Q)), device_id_type=MESH,
        )

    def ring_arrival(k):
        source = lax.rem(q + Q - k, Q)
        return pltpu.make_async_remote_copy(
            src_ref=fa.at[:, source], dst_ref=fa.at[:, source],
            send_sem=ring_send.at[k], recv_sem=ring_recv.at[k],
            device_id=(s, source), device_id_type=MESH,
        )

    def part(k):
        return pltpu.make_async_remote_copy(
            src_ref=part_out.at[k], dst_ref=part_in.at[k],
            send_sem=part_send.at[k], recv_sem=part_recv.at[k],
            device_id=(lax.rem(s + k, S), q), device_id_type=MESH,
        )

    def gather():
        @pl.when(s < pieces)
        def _():
            for face, slab, plane in holders:
                @pl.when(s != slab)
                def _():
                    pltpu.make_async_remote_copy(
                        src_ref=fa.at[face, q], dst_ref=fa.at[face, q],
                        send_sem=piece_send.at[face, 0], recv_sem=piece_recv.at[face],
                        device_id=(slab, q), device_id_type=MESH,
                    ).wait_recv()
            for k in range(1, Q):
                ring(k).start()

    def finish():
        @pl.when(s < pieces)
        def _():
            for k in range(1, Q):
                ring_arrival(k).wait_recv()
            for face in range(2):
                for a in range(Q):
                    for b in range(tiles_z):
                        t = (face * Q + a) * tiles_z + b
                        rows_buf[pl.ds(t * R, R), :] = fa[face, a, :, pl.ds(b * TILE, TILE)]
            parts = jnp.concatenate(split3(rows_buf[...]), axis=1)
            group = 4 if S % 4 == 0 else S
            for g in reversed(range(S // group)):
                sums = dot(hot_buf[pl.ds(g * group * TILE, group * TILE), :], parts)
                sums = sums[:, :TILE] + (sums[:, TILE:2 * TILE] + sums[:, 2 * TILE:])
                for k in range(g * group, (g + 1) * group):
                    part_out[k] = sums[(k - g * group) * TILE:(k - g * group + 1) * TILE]
                    if k > 0:
                        part(k).start()

        total = None
        if pieces == S:
            total = part_out[0]
            for k in range(1, S):
                part(k).wait_recv()
                total = total + part_in[k]
            parent[0] = total
        else:
            parent[...] = jnp.zeros_like(parent)

            @pl.when(s < pieces)
            def _():
                parent[0] = part_out[0]
            for k in range(1, S):
                @pl.when(lax.rem(s + S - k, S) < pieces)
                def _():
                    part(k).wait_recv()
                    parent[0] += part_in[k]

        for face, slab, plane in holders:
            @pl.when(s == slab)
            def _():
                for k in range(pieces):
                    if k != slab:
                        piece(face, plane, k).wait_send()

        @pl.when(s < pieces)
        def _():
            for k in range(1, Q):
                ring(k).wait_send()
            for k in range(1, S):
                part(k).wait_send()

    return scatter, tables, gather, finish


def cycle_kernel(
    S, Q, pieces, cot, goal, rhs, parent,
    f0, f1, f2, g3, m0, m1, m2, m3, c0, c1, gc, bm, n0, n1, gm, bf, h0, h1,
    fa, rows_buf, part_out, part_in, hot_buf,
    load_sem, send_sem, recv_sem, piece_send, piece_recv, ring_send, ring_recv, part_send, part_recv,
):
    s, q = lax.axis_index("slab"), lax.axis_index("pencil")
    has = [s > 0, s < S - 1, q > 0, q < Q - 1]
    corners = ((0, 2), (1, 3), (0, 3), (1, 2))
    has += [jnp.logical_and(has[i], has[j]) for i, j in corners]
    side_s, side_q = (lax.max(s - 1, 0), lax.min(s + 1, S - 1)), (lax.max(q - 1, 0), lax.min(q + 1, Q - 1))
    peers = [(side_s[0], q), (side_s[1], q), (s, side_q[0]), (s, side_q[1])]
    peers += [(side_s[i], side_q[j - 2]) for i, j in corners]
    NX, NYL, NZL = cot.shape
    scatter, tables, gather, finish_faces = face_steps(
        s, q, S, Q, pieces, goal, rhs, parent, fa, rows_buf, part_out, part_in,
        hot_buf, piece_send, piece_recv, ring_send, ring_recv, part_send, part_recv)

    load = pltpu.make_async_copy(cot, f0.at[pl.ds(1, NX), pl.ds(EDGE, NYL)], load_sem)
    load.start()

    barrier = pltpu.get_barrier_semaphore()
    for k in range(1, S):
        pl.semaphore_signal(
            barrier, inc=1, device_id=(lax.rem(s + k, S), q), device_id_type=MESH)
    for k in range(1, Q):
        pl.semaphore_signal(
            barrier, inc=1, device_id=(s, lax.rem(q + k, Q)), device_id_type=MESH)
    for d in range(4, 8):
        @pl.when(has[d])
        def _():
            pl.semaphore_signal(barrier, inc=1, device_id=peers[d], device_id_type=MESH)
    pl.semaphore_wait(barrier, S + Q - 2 + sum(h.astype(jnp.int32) for h in has[4:]))

    def sizes(buf):
        return buf.shape[0] - 2, buf.shape[1] - 2 * EDGE, buf.shape[2]

    def wide(buf):
        return buf is gc or buf is gm

    def sides(buf):
        return range(8) if wide(buf) else range(4)

    def chunks(buf, d):
        return CHUNKS if d < 2 and sizes(buf)[0] > 2 else 1

    def regions(buf, c=0, n=1):
        nx, ny, _ = sizes(buf)
        own_x, own_y = pl.ds(1, nx), pl.ds(EDGE + c * (ny // n), ny // n)
        k = EDGE
        src_x, halo_x = (1, nx), (0, nx + 1)
        src_y = (pl.ds(EDGE, k), pl.ds(EDGE + ny - k, k))
        halo_y = (pl.ds(EDGE - k, k), pl.ds(EDGE + ny, k))
        src = [buf.at[1, own_y], buf.at[nx, own_y], buf.at[own_x, src_y[0]], buf.at[own_x, src_y[1]]]
        halo = [buf.at[0, own_y], buf.at[nx + 1, own_y], buf.at[own_x, halo_y[0]], buf.at[own_x, halo_y[1]]]
        if wide(buf):
            src += [buf.at[src_x[i], src_y[j - 2]] for i, j in corners]
            halo += [buf.at[halo_x[i], halo_y[j - 2]] for i, j in corners]
        return src, halo

    def copy(rnd, buf, d, c):
        src, halo = regions(buf, c, chunks(buf, d))
        return pltpu.make_async_remote_copy(
            src_ref=src[d], dst_ref=halo[d ^ 1],
            send_sem=send_sem.at[rnd, d, c], recv_sem=recv_sem.at[rnd, d ^ 1, c],
            device_id=peers[d], device_id_type=MESH,
        )

    sent = {}

    def start(rnd, buf, d, c=None):
        sent[rnd] = buf

        @pl.when(has[d])
        def _():
            for i in range(chunks(buf, d)) if c is None else (c,):
                copy(rnd, buf, d, i).start()

    def arrive(rnd, buf, d, c=None):
        n = chunks(buf, d)

        @pl.when(has[d])
        def _():
            for i in range(n) if c is None else (c,):
                src, halo = regions(buf, i, n)
                pltpu.make_async_remote_copy(
                    src_ref=src[d ^ 1], dst_ref=halo[d],
                    send_sem=send_sem.at[rnd, d, i], recv_sem=recv_sem.at[rnd, d, i],
                    device_id=peers[d], device_id_type=MESH,
                ).wait_recv()

    def clear(buf):
        _, halo = regions(buf)
        for d in sides(buf):
            @pl.when(jnp.logical_not(has[d]))
            def _():
                halo[d][...] = jnp.zeros(halo[d].shape, jnp.float32)

    def neighbours(buf, x, r0, rows, before=EDGE, after=EDGE):
        z = buf.shape[2]
        first = r0 + EDGE - before
        count = before + rows + after
        big = buf[x, pl.ds(first, count), :]
        v = big[before:before + rows]
        nb = buf[x - 1, pl.ds(first + before, rows), :] + buf[x + 1, pl.ds(first + before, rows), :]
        nb = nb + pltpu.roll(big, 1, 0)[before:before + rows]
        nb = nb + pltpu.roll(big, count - 1, 0)[before:before + rows]
        lane = lax.broadcasted_iota(jnp.int32, (rows, z), 1)
        nb = nb + jnp.where(lane == 0, 0.0, pltpu.roll(v, 1, 1))
        nb = nb + jnp.where(lane == z - 1, 0.0, pltpu.roll(v, z - 1, 1))
        return v, nb

    def plane_op(buf, x_first, x_count, body):
        ny = sizes(buf)[1]
        rows = min(32, ny)
        per = ny // rows

        def step(i, _):
            body(x_first + i // per, pl.multiple_of((i % per) * rows, rows), rows)
            return 0
        lax.fori_loop(0, x_count * per, step, 0)

    def sweep(rnd, buf, finish, out_rnd=None, out=None, edge_first=None, between=None):
        nx, ny, _ = sizes(buf)

        def body(x, r0, rows):
            v, nb = neighbours(buf, x, r0, rows)
            finish(x, r0, rows, v, nb)

        def wait(d, c=None):
            if rnd is not None:
                arrive(rnd, buf, d, c)

        def send(d, c=None):
            if out is not None:
                start(out_rnd, out, d, c)
        if out is not None:
            clear(out)
        wait(2)
        wait(3)
        if edge_first is not None:
            for d, x in ((0, 1), (1, nx)):
                @pl.when(jnp.logical_not(has[d]))
                def _():
                    plane_op(buf, x, 1, body)
                    edge_first(d)
        if nx > 2 and rnd is not None:
            plane_op(buf, 2, nx - 2, body)
        if between is not None:
            between()
        if nx > 2:
            rows = ny // CHUNKS
            for c in range(CHUNKS):
                for d, x in ((0, 1), (1, nx)):
                    if edge_first is not None:
                        @pl.when(has[d])
                        def _():
                            wait(d, c)
                            body(x, c * rows, rows)
                    else:
                        wait(d, c)
                        body(x, c * rows, rows)
                    send(d, c)
            if rnd is None:
                plane_op(buf, 2, nx - 2, body)
        elif nx == 2:
            for d in range(2):
                wait(d)
                plane_op(buf, 1 + d, 1, body)
                send(d)
        else:
            wait(0)
            wait(1)
            plane_op(buf, 1, 1, body)
            send(0)
            send(1)
        if out is not None:
            for d in sides(out):
                if d >= 2:
                    send(d)

    def put(out, x, r0, rows, value):
        out[x, pl.ds(r0 + EDGE, rows), :] = value

    def own(buf, x, r0, rows):
        return buf[x, pl.ds(r0 + EDGE, rows), :]

    def smooth_to(out):
        def finish(x, r0, rows, v, nb):
            put(out, x, r0, rows, (1.0 - W) * v + (W / 6.0) * nb)
        return finish

    def restrict(src, dst):
        x, y, z = sizes(src)
        clear(dst)
        parts = []
        for j in range(x // 2):
            parts += split3(own(src, 2 * j + 1, 0, y) + own(src, 2 * j + 2, 0, y))
        half = dot(jnp.concatenate(parts, axis=0), pair_table(z, z // 2, 0, False))
        sy = pair_table(y, y // 2, 0, True)
        for j in range(x // 2):
            both = half[3 * j * y:(3 * j + 1) * y]
            both = both + (half[(3 * j + 1) * y:(3 * j + 2) * y] + half[(3 * j + 2) * y:(3 * j + 3) * y])
            hi, mid, lo = split3(both)
            put(dst, 1 + j, 0, y // 2, dot(sy, hi) + (dot(sy, mid) + dot(sy, lo)))

    def prolong(src, dst):
        nx, ny, z = sizes(src)
        py = pair_table(2 * ny + 2 * EDGE, ny + 2 * EDGE, EDGE, False)
        pz = pair_table(2 * z, z, 0, True)
        for j in range(nx + 2):
            tall = [dot(py, part).astype(jnp.bfloat16) for part in split3(src[j])]
            n = tall[0].shape[0]
            both = dot(jnp.concatenate(tall, axis=0), pz)
            value = 0.125 * (both[:n] + (both[n:2 * n] + both[2 * n:]))
            dst[2 * j] = value
            dst[2 * j + 1] = value

    def correct(back, old, out, scale):
        nx, ny, _ = sizes(out)

        def body(x, r0, rows, before=EDGE, after=EDGE):
            v, nb = neighbours(back, x + 1, r0, rows, before, after)
            put(out, x, r0, rows, own(old, x, r0, rows) - scale * (6.0 * v - nb))
        clear(out)
        plane_op(out, 1, nx, body)
        for d, x in ((0, 0), (1, nx + 1)):
            @pl.when(has[d])
            def _():
                plane_op(out, x, 1, body)
        for d, r0, before, after in ((2, -EDGE, 0, EDGE), (3, ny, EDGE, 0)):
            @pl.when(has[d])
            def _():
                for x in range(1, nx + 1):
                    body(x, r0, EDGE, before, after)

    def send_all(rnd, buf):
        for d in sides(buf):
            start(rnd, buf, d)

    def arrive_all(rnd, buf):
        for d in sides(buf):
            arrive(rnd, buf, d)

    def send_early(c):
        start(12, g3, 0, c)
        start(12, g3, 1, c)

    clear(f0)
    load.wait()
    send_all(0, f0)
    tables()
    sweep(0, f0, smooth_to(f1), 1, f1)
    sweep(1, f1, smooth_to(f2), 2, f2)
    sweep(2, f2, smooth_to(g3))
    restrict(g3, m0)
    send_all(3, m0)
    send_early(0)
    start(12, g3, 2)
    start(12, g3, 3)
    sweep(3, m0, smooth_to(m1), 4, m1)
    send_early(1)
    sweep(4, m1, smooth_to(m2), 5, m2)
    send_early(2)
    sweep(5, m2, smooth_to(m3))
    restrict(m3, c0)
    send_all(6, c0)
    send_all(9, m3)
    sweep(6, c0, smooth_to(c1), 7, c1)
    send_early(3)

    def coarse_total(x, r0, rows, v, nb):
        value = (1.0 - W) * v + (W / 6.0) * nb
        put(gc, x, r0, rows, coefficient(2) * (own(c0, x, r0, rows) + own(c1, x, r0, rows) + value))
    sweep(7, c1, coarse_total, 8, gc)
    arrive_all(8, gc)
    prolong(gc, bm)
    arrive_all(9, m3)
    correct(bm, m3, n0, 0.25)
    sweep(None, n0, smooth_to(n1), 10, n1)

    def medium_total(x, r0, rows, v, nb):
        value = (1.0 - W) * v + (W / 6.0) * nb
        total = own(m0, x, r0, rows) + own(m1, x, r0, rows) + own(m2, x, r0, rows)
        total = total + own(n0, x, r0, rows) + v + value
        put(gm, x, r0, rows, coefficient(1) * total + own(bm, x + 1, r0, rows))
    sweep(10, n1, medium_total, 11, gm)
    arrive_all(11, gm)
    prolong(gm, bf)
    arrive_all(12, g3)
    correct(bf, g3, h0, 1.0)
    sweep(None, h0, smooth_to(h1), 13, h1)

    def first_terms(x, r0, rows):
        total = own(f0, x, r0, rows) + own(f1, x, r0, rows) + own(f2, x, r0, rows)
        total = total + own(h0, x, r0, rows)
        rhs[x - 1, pl.ds(r0, rows), :] = coefficient(0) * total + own(bf, x + 1, r0, rows)
    plane_op(h0, 1, NX, first_terms)

    def last_terms(x, r0, rows, v, nb):
        value = (1.0 - W) * v + (W / 6.0) * nb
        before = rhs[x - 1, pl.ds(r0, rows), :]
        rhs[x - 1, pl.ds(r0, rows), :] = before + coefficient(0) * (v + value)
    sweep(13, h1, last_terms, edge_first=scatter, between=gather)
    finish_faces()
    for rnd, buf in sent.items():
        for d in sides(buf):
            @pl.when(has[d])
            def _():
                for c in range(chunks(buf, d)):
                    copy(rnd, buf, d, c).wait_send()


def run_cycle(cotangent, seg_rows, owners, offsets):
    S, Q = lax.axis_size("slab"), lax.axis_size("pencil")
    x, y, z = cotangent.shape
    pieces = min(S, y // EDGE)
    R = y // pieces
    targets = source_rows(seg_rows, owners, offsets, TILE)
    first = jnp.minimum(lax.axis_index("slab"), pieces - 1) * R
    goal = lax.dynamic_slice_in_dim(targets, first, R, axis=1).reshape(1, -1)

    def padded(level, deep=1):
        k = 2**level
        return pltpu.VMEM((x // k + 2 * deep, y // k + 2 * EDGE, z // k), jnp.float32)
    scratch = [padded(0)] * 4 + [padded(1)] * 4 + [padded(2)] * 3
    scratch += [padded(1, 2)] + [padded(1)] * 3 + [padded(0, 2)] + [padded(0)] * 2
    scratch += [
        pltpu.VMEM((2, Q, R, z), jnp.float32),
        pltpu.VMEM((goal.shape[1], TILE), jnp.float32),
        pltpu.VMEM((S, TILE, TILE), jnp.float32),
        pltpu.VMEM((S, TILE, TILE), jnp.float32),
        pltpu.VMEM((S * TILE, goal.shape[1]), jnp.bfloat16),
        pltpu.SemaphoreType.DMA,
        pltpu.SemaphoreType.DMA((ROUNDS, 8, CHUNKS)),
        pltpu.SemaphoreType.DMA((ROUNDS, 8, CHUNKS)),
        pltpu.SemaphoreType.DMA((2, pieces)),
        pltpu.SemaphoreType.DMA((2,)),
        pltpu.SemaphoreType.DMA((Q,)),
        pltpu.SemaphoreType.DMA((Q,)),
        pltpu.SemaphoreType.DMA((S,)),
        pltpu.SemaphoreType.DMA((S,)),
    ]
    return pl.pallas_call(
        functools.partial(cycle_kernel, S, Q, pieces),
        out_shape=(
            jax.ShapeDtypeStruct(cotangent.shape, jnp.float32),
            jax.ShapeDtypeStruct((1, TILE, TILE), jnp.float32),
        ),
        in_specs=[pl.BlockSpec(memory_space=pl.ANY), pl.BlockSpec(memory_space=pltpu.VMEM)],
        out_specs=(pl.BlockSpec(memory_space=pltpu.VMEM), pl.BlockSpec(memory_space=pltpu.VMEM)),
        scratch_shapes=scratch,
        compiler_params=pltpu.CompilerParams(
            collective_id=0, has_side_effects=True, vmem_limit_bytes=48 * 2**20
        ),
        name="vcycle",
    )(cotangent, goal)


def source_rows(seg_rows, owners, offsets, tile_size):
    starts = jnp.cumsum(seg_rows, axis=1) - seg_rows
    position = jnp.arange(tile_size, dtype=jnp.int32)[None, None, :]
    inside = (position >= starts[:, :, None]) & (position < (starts + seg_rows)[:, :, None])
    value = owners[:, :, None] * tile_size + offsets[:, :, None] + position - starts[:, :, None]
    return jnp.sum(jnp.where(inside, value, 0), axis=1)


def shards(cotangent, seg_rows, owners, offsets):
    rhs_grad, parent_grad = run_cycle(cotangent, seg_rows, owners, offsets)
    return (rhs_grad, parent_grad)


def solution(mesh):
    return jax.shard_map(
        shards,
        mesh=mesh,
        in_specs=(P("slab", "pencil", None), P(), P(), P()),
        out_specs=(P("slab", "pencil", None), P(("slab", "pencil"), None, None)),
        check_vma=False,
    )
```

```python
import functools
import jax
import jax.numpy as jnp
from jax import lax
from jax.experimental import pallas as pl
from jax.experimental.pallas import tpu as pltpu
from jax.sharding import PartitionSpec as P

TILE = 128
W = 2.0 / 3.0
EDGE = 8
ROUNDS = 14
CHUNKS = 4
MESH = pl.DeviceIdType.MESH


def coefficient(level):
    return W * 4.0**level / 6.0


def split3(x):
    hi = x.astype(jnp.bfloat16)
    rest = x - hi.astype(jnp.float32)
    mid = rest.astype(jnp.bfloat16)
    lo = (rest - mid.astype(jnp.float32)).astype(jnp.bfloat16)
    return hi, mid, lo


def dot(x, y):
    return jnp.dot(x, y, preferred_element_type=jnp.float32)


def pair_table(fine, coarse, shift, transposed):
    shape = (fine, coarse) if not transposed else (coarse, fine)
    f = lax.broadcasted_iota(jnp.int32, shape, 1 if transposed else 0)
    c = lax.broadcasted_iota(jnp.int32, shape, 0 if transposed else 1)
    return (((f + shift) // 2) == c).astype(jnp.float32).astype(jnp.bfloat16)


def face_steps(
    s, q, S, Q, pieces, goal, rhs, parent, fa, rows_buf, part_out, part_in,
    hot_buf, piece_send, piece_recv, ring_send, ring_recv, part_send, part_recv,
):
    NX, NYL, NZL = rhs.shape
    R = NYL // pieces
    tiles_z = NZL // TILE
    holders = ((0, 0, 0), (1, S - 1, NX - 1))

    def piece(face, plane, k):
        return pltpu.make_async_remote_copy(
            src_ref=rhs.at[plane, pl.ds(k * R, R)], dst_ref=fa.at[face, q],
            send_sem=piece_send.at[face, k], recv_sem=piece_recv.at[face],
            device_id=(k, q), device_id_type=MESH,
        )
    def scatter(d):
        face, slab, plane = holders[d]
        for k in range(pieces):
            if k != slab:
                piece(face, plane, k).start()
        if slab < pieces:
            fa[face, q] = rhs[plane, pl.ds(slab * R, R), :]

    def tables():
        local = lax.broadcasted_iota(jnp.int32, (TILE, goal.shape[1]), 0)
        for k in range(S):
            owner = lax.rem(s + k, S) * Q + q
            hot = (goal[...] - owner * TILE) == local
            hot_buf[pl.ds(k * TILE, TILE), :] = hot.astype(jnp.float32).astype(jnp.bfloat16)

    def ring(k):
        return pltpu.make_async_remote_copy(
            src_ref=fa.at[:, q], dst_ref=fa.at[:, q],
            send_sem=ring_send.at[k], recv_sem=ring_recv.at[k],
            device_id=(s, lax.rem(q + k, Q)), device_id_type=MESH,
        )

    def ring_arrival(k):
        source = lax.rem(q + Q - k, Q)
        return pltpu.make_async_remote_copy(
            src_ref=fa.at[:, source], dst_ref=fa.at[:, source],
            send_sem=ring_send.at[k], recv_sem=ring_recv.at[k],
            device_id=(s, source), device_id_type=MESH,
        )

    def part(k):
        return pltpu.make_async_remote_copy(
            src_ref=part_out.at[k], dst_ref=part_in.at[k],
            send_sem=part_send.at[k], recv_sem=part_recv.at[k],
            device_id=(lax.rem(s + k, S), q), device_id_type=MESH,
        )

    def gather():
        @pl.when(s < pieces)
        def _():
            for face, slab, plane in holders:
                @pl.when(s != slab)
                def _():
                    pltpu.make_async_remote_copy(
                        src_ref=fa.at[face, q], dst_ref=fa.at[face, q],
                        send_sem=piece_send.at[face, 0], recv_sem=piece_recv.at[face],
                        device_id=(slab, q), device_id_type=MESH,
                    ).wait_recv()
            for k in range(1, Q):
                ring(k).start()

    def finish():
        @pl.when(s < pieces)
        def _():
            for k in range(1, Q):
                ring_arrival(k).wait_recv()
            for face in range(2):
                for a in range(Q):
                    for b in range(tiles_z):
                        t = (face * Q + a) * tiles_z + b
                        rows_buf[pl.ds(t * R, R), :] = fa[face, a, :, pl.ds(b * TILE, TILE)]
            parts = jnp.concatenate(split3(rows_buf[...]), axis=1)
            group = 4 if S % 4 == 0 else S
            for g in reversed(range(S // group)):
                sums = dot(hot_buf[pl.ds(g * group * TILE, group * TILE), :], parts)
                sums = sums[:, :TILE] + (sums[:, TILE:2 * TILE] + sums[:, 2 * TILE:])
                for k in range(g * group, (g + 1) * group):
                    part_out[k] = sums[(k - g * group) * TILE:(k - g * group + 1) * TILE]
                    if k > 0:
                        part(k).start()

        total = None
        if pieces == S:
            total = part_out[0]
            for k in range(1, S):
                part(k).wait_recv()
                total = total + part_in[k]
            parent[0] = total
        else:
            parent[...] = jnp.zeros_like(parent)

            @pl.when(s < pieces)
            def _():
                parent[0] = part_out[0]
            for k in range(1, S):
                @pl.when(lax.rem(s + S - k, S) < pieces)
                def _():
                    part(k).wait_recv()
                    parent[0] += part_in[k]

        for face, slab, plane in holders:
            @pl.when(s == slab)
            def _():
                for k in range(pieces):
                    if k != slab:
                        piece(face, plane, k).wait_send()

        @pl.when(s < pieces)
        def _():
            for k in range(1, Q):
                ring(k).wait_send()
            for k in range(1, S):
                part(k).wait_send()

    return scatter, tables, gather, finish


def cycle_kernel(
    S, Q, pieces, cot, goal, rhs, parent,
    f0, f1, f2, g3, m0, m1, m2, m3, c0, c1, gc, bm, n0, n1, gm, bf, h0, h1,
    fa, rows_buf, part_out, part_in, hot_buf,
    load_sem, send_sem, recv_sem, piece_send, piece_recv, ring_send, ring_recv, part_send, part_recv,
):
    s, q = lax.axis_index("slab"), lax.axis_index("pencil")
    has = [s > 0, s < S - 1, q > 0, q < Q - 1]
    corners = ((0, 2), (1, 3), (0, 3), (1, 2))
    has += [jnp.logical_and(has[i], has[j]) for i, j in corners]
    side_s, side_q = (lax.max(s - 1, 0), lax.min(s + 1, S - 1)), (lax.max(q - 1, 0), lax.min(q + 1, Q - 1))
    peers = [(side_s[0], q), (side_s[1], q), (s, side_q[0]), (s, side_q[1])]
    peers += [(side_s[i], side_q[j - 2]) for i, j in corners]
    NX, NYL, NZL = cot.shape
    scatter, tables, gather, finish_faces = face_steps(
        s, q, S, Q, pieces, goal, rhs, parent, fa, rows_buf, part_out, part_in,
        hot_buf, piece_send, piece_recv, ring_send, ring_recv, part_send, part_recv)

    load = pltpu.make_async_copy(cot, f0.at[pl.ds(1, NX), pl.ds(EDGE, NYL)], load_sem)
    load.start()

    barrier = pltpu.get_barrier_semaphore()
    for k in range(1, S):
        pl.semaphore_signal(
            barrier, inc=1, device_id=(lax.rem(s + k, S), q), device_id_type=MESH)
    for k in range(1, Q):
        pl.semaphore_signal(
            barrier, inc=1, device_id=(s, lax.rem(q + k, Q)), device_id_type=MESH)
    for d in range(4, 8):
        @pl.when(has[d])
        def _():
            pl.semaphore_signal(barrier, inc=1, device_id=peers[d], device_id_type=MESH)
    pl.semaphore_wait(barrier, S + Q - 2 + sum(h.astype(jnp.int32) for h in has[4:]))

    def sizes(buf):
        return buf.shape[0] - 2, buf.shape[1] - 2 * EDGE, buf.shape[2]

    def wide(buf):
        return buf is gc or buf is gm

    def sides(buf):
        return range(8) if wide(buf) else range(4)

    def chunks(buf, d):
        return CHUNKS if d < 2 and sizes(buf)[0] > 2 else 1

    def regions(buf, c=0, n=1):
        nx, ny, _ = sizes(buf)
        own_x, own_y = pl.ds(1, nx), pl.ds(EDGE + c * (ny // n), ny // n)
        k = EDGE
        src_x, halo_x = (1, nx), (0, nx + 1)
        src_y = (pl.ds(EDGE, k), pl.ds(EDGE + ny - k, k))
        halo_y = (pl.ds(EDGE - k, k), pl.ds(EDGE + ny, k))
        src = [buf.at[1, own_y], buf.at[nx, own_y], buf.at[own_x, src_y[0]], buf.at[own_x, src_y[1]]]
        halo = [buf.at[0, own_y], buf.at[nx + 1, own_y], buf.at[own_x, halo_y[0]], buf.at[own_x, halo_y[1]]]
        if wide(buf):
            src += [buf.at[src_x[i], src_y[j - 2]] for i, j in corners]
            halo += [buf.at[halo_x[i], halo_y[j - 2]] for i, j in corners]
        return src, halo

    def copy(rnd, buf, d, c):
        src, halo = regions(buf, c, chunks(buf, d))
        if buf is f0:
            n = NYL // chunks(buf, d)
            src = (
                cot.at[0, pl.ds(c * n, n)], cot.at[NX - 1, pl.ds(c * n, n)],
                cot.at[:, pl.ds(0, EDGE)], cot.at[:, pl.ds(NYL - EDGE, EDGE)],
            )
        return pltpu.make_async_remote_copy(
            src_ref=src[d], dst_ref=halo[d ^ 1],
            send_sem=send_sem.at[rnd, d, c], recv_sem=recv_sem.at[rnd, d ^ 1, c],
            device_id=peers[d], device_id_type=MESH,
        )

    sent = {}

    def start(rnd, buf, d, c=None):
        sent[rnd] = buf

        @pl.when(has[d])
        def _():
            for i in range(chunks(buf, d)) if c is None else (c,):
                copy(rnd, buf, d, i).start()

    def arrive(rnd, buf, d, c=None):
        n = chunks(buf, d)

        @pl.when(has[d])
        def _():
            for i in range(n) if c is None else (c,):
                src, halo = regions(buf, i, n)
                pltpu.make_async_remote_copy(
                    src_ref=src[d ^ 1], dst_ref=halo[d],
                    send_sem=send_sem.at[rnd, d, i], recv_sem=recv_sem.at[rnd, d, i],
                    device_id=peers[d], device_id_type=MESH,
                ).wait_recv()

    def clear(buf):
        _, halo = regions(buf)
        for d in sides(buf):
            @pl.when(jnp.logical_not(has[d]))
            def _():
                halo[d][...] = jnp.zeros(halo[d].shape, jnp.float32)

    def neighbours(buf, x, r0, rows, before=EDGE, after=EDGE):
        z = buf.shape[2]
        first = r0 + EDGE - before
        count = before + rows + after
        big = buf[x, pl.ds(first, count), :]
        v = big[before:before + rows]
        nb = buf[x - 1, pl.ds(first + before, rows), :] + buf[x + 1, pl.ds(first + before, rows), :]
        nb = nb + pltpu.roll(big, 1, 0)[before:before + rows]
        nb = nb + pltpu.roll(big, count - 1, 0)[before:before + rows]
        lane = lax.broadcasted_iota(jnp.int32, (rows, z), 1)
        nb = nb + jnp.where(lane == 0, 0.0, pltpu.roll(v, 1, 1))
        nb = nb + jnp.where(lane == z - 1, 0.0, pltpu.roll(v, z - 1, 1))
        return v, nb

    def plane_op(buf, x_first, x_count, body):
        ny = sizes(buf)[1]
        rows = min(16, ny)
        per = ny // rows

        def step(i, _):
            body(x_first + i // per, pl.multiple_of((i % per) * rows, rows), rows)
            return 0
        lax.fori_loop(0, x_count * per, step, 0, unroll=2)

    def sweep(rnd, buf, finish, out_rnd=None, out=None, edge_first=None, between=None):
        nx, ny, _ = sizes(buf)

        def body(x, r0, rows):
            v, nb = neighbours(buf, x, r0, rows)
            finish(x, r0, rows, v, nb)

        def halves(x, r0, rows):
            for r in range(r0, r0 + rows, 16):
                body(x, r, 16)

        def wait(d, c=None):
            if rnd is not None:
                arrive(rnd, buf, d, c)

        def send(d, c=None):
            if out is not None:
                start(out_rnd, out, d, c)
        if out is not None:
            clear(out)
        wait(2)
        wait(3)
        if edge_first is not None:
            for d, x in ((0, 1), (1, nx)):
                @pl.when(jnp.logical_not(has[d]))
                def _():
                    plane_op(buf, x, 1, body)
                    edge_first(d)
        if nx > 2 and rnd is not None:
            plane_op(buf, 2, nx - 2, body)
        if between is not None:
            between()
        if nx > 2:
            rows = ny // CHUNKS
            for c in range(CHUNKS):
                for d, x in ((0, 1), (1, nx)):
                    if edge_first is not None:
                        @pl.when(has[d])
                        def _():
                            wait(d, c)
                            halves(x, c * rows, rows)
                    else:
                        wait(d, c)
                        halves(x, c * rows, rows)
                    send(d, c)
            if rnd is None:
                plane_op(buf, 2, nx - 2, body)
        elif nx == 2:
            for d in range(2):
                wait(d)
                plane_op(buf, 1 + d, 1, body)
                send(d)
        else:
            wait(0)
            wait(1)
            plane_op(buf, 1, 1, body)
            send(0)
            send(1)
        if out is not None:
            for d in sides(out):
                if d >= 2:
                    send(d)

    def put(out, x, r0, rows, value):
        out[x, pl.ds(r0 + EDGE, rows), :] = value

    def own(buf, x, r0, rows):
        return buf[x, pl.ds(r0 + EDGE, rows), :]

    def smooth_to(out):
        def finish(x, r0, rows, v, nb):
            put(out, x, r0, rows, (1.0 - W) * v + (W / 6.0) * nb)
        return finish

    def restrict(src, dst):
        x, y, z = sizes(src)
        clear(dst)
        parts = []
        for j in range(x // 2):
            parts += split3(own(src, 2 * j + 1, 0, y) + own(src, 2 * j + 2, 0, y))
        half = dot(jnp.concatenate(parts, axis=0), pair_table(z, z // 2, 0, False))
        sy = pair_table(y, y // 2, 0, True)
        for j in range(x // 2):
            both = half[3 * j * y:(3 * j + 1) * y]
            both = both + (half[(3 * j + 1) * y:(3 * j + 2) * y] + half[(3 * j + 2) * y:(3 * j + 3) * y])
            hi, mid, lo = split3(both)
            put(dst, 1 + j, 0, y // 2, dot(sy, hi) + (dot(sy, mid) + dot(sy, lo)))

    def prolong(src, dst):
        nx, ny, z = sizes(src)
        py = pair_table(2 * ny + 2 * EDGE, ny + 2 * EDGE, EDGE, False)
        pz = pair_table(2 * z, z, 0, True)
        for j in range(nx + 2):
            tall = [dot(py, part).astype(jnp.bfloat16) for part in split3(src[j])]
            n = tall[0].shape[0]
            both = dot(jnp.concatenate(tall, axis=0), pz)
            value = 0.125 * (both[:n] + (both[n:2 * n] + both[2 * n:]))
            dst[2 * j] = value
            dst[2 * j + 1] = value

    def correct(back, old, out, scale):
        nx, ny, _ = sizes(out)

        def body(x, r0, rows, before=EDGE, after=EDGE):
            v, nb = neighbours(back, x + 1, r0, rows, before, after)
            put(out, x, r0, rows, own(old, x, r0, rows) - scale * (6.0 * v - nb))
        clear(out)
        plane_op(out, 1, nx, body)
        for d, x in ((0, 0), (1, nx + 1)):
            @pl.when(has[d])
            def _():
                plane_op(out, x, 1, body)
        for d, r0, before, after in ((2, -EDGE, 0, EDGE), (3, ny, EDGE, 0)):
            @pl.when(has[d])
            def _():
                for x in range(1, nx + 1):
                    body(x, r0, EDGE, before, after)

    def send_all(rnd, buf):
        for d in sides(buf):
            start(rnd, buf, d)

    def arrive_all(rnd, buf):
        for d in sides(buf):
            arrive(rnd, buf, d)

    def send_early(c):
        start(12, g3, 0, c)
        start(12, g3, 1, c)

    send_all(0, f0)
    clear(f0)
    tables()
    load.wait()
    sweep(0, f0, smooth_to(f1), 1, f1)
    sweep(1, f1, smooth_to(f2), 2, f2)
    sweep(2, f2, smooth_to(g3))
    restrict(g3, m0)
    send_all(3, m0)
    send_early(0)
    start(12, g3, 2)
    start(12, g3, 3)
    sweep(3, m0, smooth_to(m1), 4, m1)
    send_early(1)
    sweep(4, m1, smooth_to(m2), 5, m2)
    send_early(2)
    sweep(5, m2, smooth_to(m3))
    restrict(m3, c0)
    send_all(6, c0)
    send_all(9, m3)
    sweep(6, c0, smooth_to(c1), 7, c1)
    send_early(3)

    def coarse_total(x, r0, rows, v, nb):
        value = (1.0 - W) * v + (W / 6.0) * nb
        put(gc, x, r0, rows, coefficient(2) * (own(c0, x, r0, rows) + own(c1, x, r0, rows) + value))
    sweep(7, c1, coarse_total, 8, gc)
    arrive_all(8, gc)
    prolong(gc, bm)
    arrive_all(9, m3)
    correct(bm, m3, n0, 0.25)
    sweep(None, n0, smooth_to(n1), 10, n1)

    def medium_total(x, r0, rows, v, nb):
        value = (1.0 - W) * v + (W / 6.0) * nb
        total = own(m0, x, r0, rows) + own(m1, x, r0, rows) + own(m2, x, r0, rows)
        total = total + own(n0, x, r0, rows) + v + value
        put(gm, x, r0, rows, coefficient(1) * total + own(bm, x + 1, r0, rows))
    sweep(10, n1, medium_total, 11, gm)
    arrive_all(11, gm)
    prolong(gm, bf)
    arrive_all(12, g3)
    correct(bf, g3, h0, 1.0)
    sweep(None, h0, smooth_to(h1), 13, h1)

    def first_terms(x, r0, rows):
        total = own(f0, x, r0, rows) + own(f1, x, r0, rows) + own(f2, x, r0, rows)
        total = total + own(h0, x, r0, rows)
        rhs[x - 1, pl.ds(r0, rows), :] = coefficient(0) * total + own(bf, x + 1, r0, rows)
    plane_op(h0, 1, NX, first_terms)

    def last_terms(x, r0, rows, v, nb):
        value = (1.0 - W) * v + (W / 6.0) * nb
        before = rhs[x - 1, pl.ds(r0, rows), :]
        rhs[x - 1, pl.ds(r0, rows), :] = before + coefficient(0) * (v + value)
    sweep(13, h1, last_terms, edge_first=scatter, between=gather)
    finish_faces()
    for rnd, buf in sent.items():
        for d in sides(buf):
            @pl.when(has[d])
            def _():
                for c in range(chunks(buf, d)):
                    copy(rnd, buf, d, c).wait_send()


def run_cycle(cotangent, seg_rows, owners, offsets):
    S, Q = lax.axis_size("slab"), lax.axis_size("pencil")
    x, y, z = cotangent.shape
    pieces = min(S, y // EDGE)
    R = y // pieces
    targets = source_rows(seg_rows, owners, offsets, TILE)
    first = jnp.minimum(lax.axis_index("slab"), pieces - 1) * R
    goal = lax.dynamic_slice_in_dim(targets, first, R, axis=1).reshape(1, -1)

    def padded(level, deep=1):
        k = 2**level
        return pltpu.VMEM((x // k + 2 * deep, y // k + 2 * EDGE, z // k), jnp.float32)
    scratch = [padded(0)] * 4 + [padded(1)] * 4 + [padded(2)] * 3
    scratch += [padded(1, 2)] + [padded(1)] * 3 + [padded(0, 2)] + [padded(0)] * 2
    scratch += [
        pltpu.VMEM((2, Q, R, z), jnp.float32),
        pltpu.VMEM((goal.shape[1], TILE), jnp.float32),
        pltpu.VMEM((S, TILE, TILE), jnp.float32),
        pltpu.VMEM((S, TILE, TILE), jnp.float32),
        pltpu.VMEM((S * TILE, goal.shape[1]), jnp.bfloat16),
        pltpu.SemaphoreType.DMA,
        pltpu.SemaphoreType.DMA((ROUNDS, 8, CHUNKS)),
        pltpu.SemaphoreType.DMA((ROUNDS, 8, CHUNKS)),
        pltpu.SemaphoreType.DMA((2, pieces)),
        pltpu.SemaphoreType.DMA((2,)),
        pltpu.SemaphoreType.DMA((Q,)),
        pltpu.SemaphoreType.DMA((Q,)),
        pltpu.SemaphoreType.DMA((S,)),
        pltpu.SemaphoreType.DMA((S,)),
    ]
    return pl.pallas_call(
        functools.partial(cycle_kernel, S, Q, pieces),
        out_shape=(
            jax.ShapeDtypeStruct(cotangent.shape, jnp.float32),
            jax.ShapeDtypeStruct((1, TILE, TILE), jnp.float32),
        ),
        in_specs=[pl.BlockSpec(memory_space=pl.ANY), pl.BlockSpec(memory_space=pltpu.VMEM)],
        out_specs=(pl.BlockSpec(memory_space=pltpu.VMEM), pl.BlockSpec(memory_space=pltpu.VMEM)),
        scratch_shapes=scratch,
        compiler_params=pltpu.CompilerParams(
            collective_id=0, has_side_effects=True, vmem_limit_bytes=60 * 2**20
        ),
        name="vcycle",
    )(cotangent, goal)


def source_rows(seg_rows, owners, offsets, tile_size):
    starts = jnp.cumsum(seg_rows, axis=1) - seg_rows
    position = jnp.arange(tile_size, dtype=jnp.int32)[None, None, :]
    inside = (position >= starts[:, :, None]) & (position < (starts + seg_rows)[:, :, None])
    value = owners[:, :, None] * tile_size + offsets[:, :, None] + position - starts[:, :, None]
    return jnp.sum(jnp.where(inside, value, 0), axis=1)


def shards(cotangent, seg_rows, owners, offsets):
    rhs_grad, parent_grad = run_cycle(cotangent, seg_rows, owners, offsets)
    return (rhs_grad, parent_grad)


def solution(mesh):
    return jax.shard_map(
        shards,
        mesh=mesh,
        in_specs=(P("slab", "pencil", None), P(), P(), P()),
        out_specs=(P("slab", "pencil", None), P(("slab", "pencil"), None, None)),
        check_vma=False,
    )
```

```python
import functools
import jax
import jax.numpy as jnp
from jax import lax
from jax.experimental import pallas as pl
from jax.experimental.pallas import tpu as pltpu
from jax.sharding import PartitionSpec as P

TILE = 128
W = 2.0 / 3.0
EDGE = 8
ROUNDS = 14
CHUNKS = 4
MESH = pl.DeviceIdType.MESH


def coefficient(level):
    return W * 4.0**level / 6.0


def split3(x):
    hi = x.astype(jnp.bfloat16)
    rest = x - hi.astype(jnp.float32)
    mid = rest.astype(jnp.bfloat16)
    lo = (rest - mid.astype(jnp.float32)).astype(jnp.bfloat16)
    return hi, mid, lo


def dot(x, y):
    return jnp.dot(x, y, preferred_element_type=jnp.float32)


def pair_table(fine, coarse, shift, transposed):
    shape = (fine, coarse) if not transposed else (coarse, fine)
    f = lax.broadcasted_iota(jnp.int32, shape, 1 if transposed else 0)
    c = lax.broadcasted_iota(jnp.int32, shape, 0 if transposed else 1)
    return (((f + shift) // 2) == c).astype(jnp.float32).astype(jnp.bfloat16)


def face_steps(
    s, q, S, Q, pieces, goal, rhs, parent, fa, rows_buf, part_out, part_in,
    hot_buf, piece_send, piece_recv, ring_send, ring_recv, part_send, part_recv,
):
    NX, NYL, NZL = rhs.shape
    R = NYL // pieces
    tiles_z = NZL // TILE
    holders = ((0, 0, 0), (1, S - 1, NX - 1))

    def piece(face, plane, k):
        return pltpu.make_async_remote_copy(
            src_ref=rhs.at[plane, pl.ds(k * R, R)], dst_ref=fa.at[face, q],
            send_sem=piece_send.at[face, k], recv_sem=piece_recv.at[face],
            device_id=(k, q), device_id_type=MESH,
        )
    def scatter(d):
        face, slab, plane = holders[d]
        for k in range(pieces):
            if k != slab:
                piece(face, plane, k).start()
        if slab < pieces:
            fa[face, q] = rhs[plane, pl.ds(slab * R, R), :]

    def tables():
        local = lax.broadcasted_iota(jnp.int32, (TILE, goal.shape[1]), 0)
        for k in range(S):
            owner = lax.rem(s + k, S) * Q + q
            hot = (goal[...] - owner * TILE) == local
            hot_buf[pl.ds(k * TILE, TILE), :] = hot.astype(jnp.float32).astype(jnp.bfloat16)

    def ring(k):
        return pltpu.make_async_remote_copy(
            src_ref=fa.at[:, q], dst_ref=fa.at[:, q],
            send_sem=ring_send.at[k], recv_sem=ring_recv.at[k],
            device_id=(s, lax.rem(q + k, Q)), device_id_type=MESH,
        )

    def ring_arrival(k):
        source = lax.rem(q + Q - k, Q)
        return pltpu.make_async_remote_copy(
            src_ref=fa.at[:, source], dst_ref=fa.at[:, source],
            send_sem=ring_send.at[k], recv_sem=ring_recv.at[k],
            device_id=(s, source), device_id_type=MESH,
        )

    def part(k):
        return pltpu.make_async_remote_copy(
            src_ref=part_out.at[k], dst_ref=part_in.at[k],
            send_sem=part_send.at[k], recv_sem=part_recv.at[k],
            device_id=(lax.rem(s + k, S), q), device_id_type=MESH,
        )

    def gather():
        @pl.when(s < pieces)
        def _():
            for face, slab, plane in holders:
                @pl.when(s != slab)
                def _():
                    pltpu.make_async_remote_copy(
                        src_ref=fa.at[face, q], dst_ref=fa.at[face, q],
                        send_sem=piece_send.at[face, 0], recv_sem=piece_recv.at[face],
                        device_id=(slab, q), device_id_type=MESH,
                    ).wait_recv()
            for k in range(1, Q):
                ring(k).start()

    def finish():
        @pl.when(s < pieces)
        def _():
            for k in range(1, Q):
                ring_arrival(k).wait_recv()
            for face in range(2):
                for a in range(Q):
                    for b in range(tiles_z):
                        t = (face * Q + a) * tiles_z + b
                        rows_buf[pl.ds(t * R, R), :] = fa[face, a, :, pl.ds(b * TILE, TILE)]
            parts = jnp.concatenate(split3(rows_buf[...]), axis=1)
            group = 4 if S % 4 == 0 else S
            for g in reversed(range(S // group)):
                sums = dot(hot_buf[pl.ds(g * group * TILE, group * TILE), :], parts)
                sums = sums[:, :TILE] + (sums[:, TILE:2 * TILE] + sums[:, 2 * TILE:])
                for k in range(g * group, (g + 1) * group):
                    part_out[k] = sums[(k - g * group) * TILE:(k - g * group + 1) * TILE]
                    if k > 0:
                        part(k).start()

        total = None
        if pieces == S:
            total = part_out[0]
            for k in range(1, S):
                part(k).wait_recv()
                total = total + part_in[k]
            parent[0] = total
        else:
            parent[...] = jnp.zeros_like(parent)

            @pl.when(s < pieces)
            def _():
                parent[0] = part_out[0]
            for k in range(1, S):
                @pl.when(lax.rem(s + S - k, S) < pieces)
                def _():
                    part(k).wait_recv()
                    parent[0] += part_in[k]

        for face, slab, plane in holders:
            @pl.when(s == slab)
            def _():
                for k in range(pieces):
                    if k != slab:
                        piece(face, plane, k).wait_send()

        @pl.when(s < pieces)
        def _():
            for k in range(1, Q):
                ring(k).wait_send()
            for k in range(1, S):
                part(k).wait_send()

    return scatter, tables, gather, finish


def cycle_kernel(
    S, Q, pieces, cot, goal, rhs, parent,
    f0, f1, f2, g3, m0, m1, m2, m3, c0, c1, gc, bm, n0, n1, gm, bf, h0, h1,
    fa, rows_buf, part_out, part_in, hot_buf,
    load_sem, send_sem, recv_sem, piece_send, piece_recv, ring_send, ring_recv, part_send, part_recv,
):
    s, q = lax.axis_index("slab"), lax.axis_index("pencil")
    has = [s > 0, s < S - 1, q > 0, q < Q - 1]
    corners = ((0, 2), (1, 3), (0, 3), (1, 2))
    has += [jnp.logical_and(has[i], has[j]) for i, j in corners]
    side_s, side_q = (lax.max(s - 1, 0), lax.min(s + 1, S - 1)), (lax.max(q - 1, 0), lax.min(q + 1, Q - 1))
    peers = [(side_s[0], q), (side_s[1], q), (s, side_q[0]), (s, side_q[1])]
    peers += [(side_s[i], side_q[j - 2]) for i, j in corners]
    NX, NYL, NZL = cot.shape
    scatter, tables, gather, finish_faces = face_steps(
        s, q, S, Q, pieces, goal, rhs, parent, fa, rows_buf, part_out, part_in,
        hot_buf, piece_send, piece_recv, ring_send, ring_recv, part_send, part_recv)

    load = pltpu.make_async_copy(cot, f0.at[pl.ds(1, NX), pl.ds(EDGE, NYL)], load_sem)
    load.start()

    barrier = pltpu.get_barrier_semaphore()
    for k in range(1, S):
        pl.semaphore_signal(
            barrier, inc=1, device_id=(lax.rem(s + k, S), q), device_id_type=MESH)
    for k in range(1, Q):
        pl.semaphore_signal(
            barrier, inc=1, device_id=(s, lax.rem(q + k, Q)), device_id_type=MESH)
    for d in range(4, 8):
        @pl.when(has[d])
        def _():
            pl.semaphore_signal(barrier, inc=1, device_id=peers[d], device_id_type=MESH)
    pl.semaphore_wait(barrier, S + Q - 2 + sum(h.astype(jnp.int32) for h in has[4:]))

    def sizes(buf):
        return buf.shape[0] - 2, buf.shape[1] - 2 * EDGE, buf.shape[2]

    def wide(buf):
        return buf is gc or buf is gm

    def sides(buf):
        return range(8) if wide(buf) else range(4)

    def chunks(buf, d):
        return CHUNKS if d < 2 and sizes(buf)[0] > 2 else 1

    def regions(buf, c=0, n=1):
        nx, ny, _ = sizes(buf)
        own_x, own_y = pl.ds(1, nx), pl.ds(EDGE + c * (ny // n), ny // n)
        k = EDGE
        src_x, halo_x = (1, nx), (0, nx + 1)
        src_y = (pl.ds(EDGE, k), pl.ds(EDGE + ny - k, k))
        halo_y = (pl.ds(EDGE - k, k), pl.ds(EDGE + ny, k))
        src = [buf.at[1, own_y], buf.at[nx, own_y], buf.at[own_x, src_y[0]], buf.at[own_x, src_y[1]]]
        halo = [buf.at[0, own_y], buf.at[nx + 1, own_y], buf.at[own_x, halo_y[0]], buf.at[own_x, halo_y[1]]]
        if wide(buf):
            src += [buf.at[src_x[i], src_y[j - 2]] for i, j in corners]
            halo += [buf.at[halo_x[i], halo_y[j - 2]] for i, j in corners]
        return src, halo

    def copy(rnd, buf, d, c):
        src, halo = regions(buf, c, chunks(buf, d))
        return pltpu.make_async_remote_copy(
            src_ref=src[d], dst_ref=halo[d ^ 1],
            send_sem=send_sem.at[rnd, d, c], recv_sem=recv_sem.at[rnd, d ^ 1, c],
            device_id=peers[d], device_id_type=MESH,
        )

    sent = {}

    def start(rnd, buf, d, c=None):
        sent[rnd] = buf

        @pl.when(has[d])
        def _():
            for i in range(chunks(buf, d)) if c is None else (c,):
                copy(rnd, buf, d, i).start()

    def arrive(rnd, buf, d, c=None):
        n = chunks(buf, d)

        @pl.when(has[d])
        def _():
            for i in range(n) if c is None else (c,):
                src, halo = regions(buf, i, n)
                pltpu.make_async_remote_copy(
                    src_ref=src[d ^ 1], dst_ref=halo[d],
                    send_sem=send_sem.at[rnd, d, i], recv_sem=recv_sem.at[rnd, d, i],
                    device_id=peers[d], device_id_type=MESH,
                ).wait_recv()

    def clear(buf):
        _, halo = regions(buf)
        for d in sides(buf):
            @pl.when(jnp.logical_not(has[d]))
            def _():
                halo[d][...] = jnp.zeros(halo[d].shape, jnp.float32)

    def neighbours(buf, x, r0, rows, before=EDGE, after=EDGE):
        z = buf.shape[2]
        first = r0 + EDGE - before
        count = before + rows + after
        big = buf[x, pl.ds(first, count), :]
        v = big[before:before + rows]
        nb = buf[x - 1, pl.ds(first + before, rows), :] + buf[x + 1, pl.ds(first + before, rows), :]
        nb = nb + pltpu.roll(big, 1, 0)[before:before + rows]
        nb = nb + pltpu.roll(big, count - 1, 0)[before:before + rows]
        lane = lax.broadcasted_iota(jnp.int32, (rows, z), 1)
        nb = nb + jnp.where(lane == 0, 0.0, pltpu.roll(v, 1, 1))
        nb = nb + jnp.where(lane == z - 1, 0.0, pltpu.roll(v, z - 1, 1))
        return v, nb

    def plane_op(buf, x_first, x_count, body):
        ny = sizes(buf)[1]
        rows = min(32, ny)
        per = ny // rows

        def step(i, _):
            body(x_first + i // per, pl.multiple_of((i % per) * rows, rows), rows)
            return 0
        lax.fori_loop(0, x_count * per, step, 0, unroll=2)

    def sweep(rnd, buf, finish, out_rnd=None, out=None, edge_first=None, between=None):
        nx, ny, _ = sizes(buf)

        def body(x, r0, rows):
            v, nb = neighbours(buf, x, r0, rows)
            finish(x, r0, rows, v, nb)

        def wait(d, c=None):
            if rnd is not None:
                arrive(rnd, buf, d, c)

        def send(d, c=None):
            if out is not None:
                start(out_rnd, out, d, c)
        if out is not None:
            clear(out)
        wait(2)
        wait(3)
        if edge_first is not None:
            for d, x in ((0, 1), (1, nx)):
                @pl.when(jnp.logical_not(has[d]))
                def _():
                    plane_op(buf, x, 1, body)
                    edge_first(d)
        if nx > 2 and rnd is not None:
            plane_op(buf, 2, nx - 2, body)
        if between is not None:
            between()
        if nx > 2:
            rows = ny // CHUNKS
            for c in range(CHUNKS):
                for d, x in ((0, 1), (1, nx)):
                    if edge_first is not None:
                        @pl.when(has[d])
                        def _():
                            wait(d, c)
                            body(x, c * rows, rows)
                    else:
                        wait(d, c)
                        body(x, c * rows, rows)
                    send(d, c)
            if rnd is None:
                plane_op(buf, 2, nx - 2, body)
        elif nx == 2:
            for d in range(2):
                wait(d)
                plane_op(buf, 1 + d, 1, body)
                send(d)
        else:
            wait(0)
            wait(1)
            plane_op(buf, 1, 1, body)
            send(0)
            send(1)
        if out is not None:
            for d in sides(out):
                if d >= 2:
                    send(d)

    def put(out, x, r0, rows, value):
        out[x, pl.ds(r0 + EDGE, rows), :] = value

    def own(buf, x, r0, rows):
        return buf[x, pl.ds(r0 + EDGE, rows), :]

    def smooth_to(out):
        def finish(x, r0, rows, v, nb):
            put(out, x, r0, rows, (1.0 - W) * v + (W / 6.0) * nb)
        return finish

    def restrict(src, dst):
        x, y, z = sizes(src)
        clear(dst)
        parts = []
        for j in range(x // 2):
            parts += split3(own(src, 2 * j + 1, 0, y) + own(src, 2 * j + 2, 0, y))
        half = dot(jnp.concatenate(parts, axis=0), pair_table(z, z // 2, 0, False))
        sy = pair_table(y, y // 2, 0, True)
        for j in range(x // 2):
            both = half[3 * j * y:(3 * j + 1) * y]
            both = both + (half[(3 * j + 1) * y:(3 * j + 2) * y] + half[(3 * j + 2) * y:(3 * j + 3) * y])
            hi, mid, lo = split3(both)
            put(dst, 1 + j, 0, y // 2, dot(sy, hi) + (dot(sy, mid) + dot(sy, lo)))

    def prolong(src, dst):
        nx, ny, z = sizes(src)
        py = pair_table(2 * ny + 2 * EDGE, ny + 2 * EDGE, EDGE, False)
        pz = pair_table(2 * z, z, 0, True)
        for j in range(nx + 2):
            tall = [dot(py, part).astype(jnp.bfloat16) for part in split3(src[j])]
            n = tall[0].shape[0]
            both = dot(jnp.concatenate(tall, axis=0), pz)
            value = 0.125 * (both[:n] + (both[n:2 * n] + both[2 * n:]))
            dst[2 * j] = value
            dst[2 * j + 1] = value

    def correct(back, old, out, scale):
        nx, ny, _ = sizes(out)

        def body(x, r0, rows, before=EDGE, after=EDGE):
            v, nb = neighbours(back, x + 1, r0, rows, before, after)
            put(out, x, r0, rows, own(old, x, r0, rows) - scale * (6.0 * v - nb))
        clear(out)
        plane_op(out, 1, nx, body)
        for d, x in ((0, 0), (1, nx + 1)):
            @pl.when(has[d])
            def _():
                plane_op(out, x, 1, body)
        for d, r0, before, after in ((2, -EDGE, 0, EDGE), (3, ny, EDGE, 0)):
            @pl.when(has[d])
            def _():
                for x in range(1, nx + 1):
                    body(x, r0, EDGE, before, after)

    def send_all(rnd, buf):
        for d in sides(buf):
            start(rnd, buf, d)

    def arrive_all(rnd, buf):
        for d in sides(buf):
            arrive(rnd, buf, d)

    def send_early(c):
        start(12, g3, 0, c)
        start(12, g3, 1, c)

    clear(f0)
    load.wait()
    send_all(0, f0)
    tables()
    sweep(0, f0, smooth_to(f1), 1, f1)
    sweep(1, f1, smooth_to(f2), 2, f2)
    sweep(2, f2, smooth_to(g3))
    restrict(g3, m0)
    send_all(3, m0)
    send_early(0)
    start(12, g3, 2)
    start(12, g3, 3)
    sweep(3, m0, smooth_to(m1), 4, m1)
    send_early(1)
    sweep(4, m1, smooth_to(m2), 5, m2)
    send_early(2)
    sweep(5, m2, smooth_to(m3))
    restrict(m3, c0)
    send_all(6, c0)
    send_all(9, m3)
    sweep(6, c0, smooth_to(c1), 7, c1)
    send_early(3)

    def coarse_total(x, r0, rows, v, nb):
        value = (1.0 - W) * v + (W / 6.0) * nb
        put(gc, x, r0, rows, coefficient(2) * (own(c0, x, r0, rows) + own(c1, x, r0, rows) + value))
    sweep(7, c1, coarse_total, 8, gc)
    arrive_all(8, gc)
    prolong(gc, bm)
    arrive_all(9, m3)
    correct(bm, m3, n0, 0.25)
    sweep(None, n0, smooth_to(n1), 10, n1)

    def medium_total(x, r0, rows, v, nb):
        value = (1.0 - W) * v + (W / 6.0) * nb
        total = own(m0, x, r0, rows) + own(m1, x, r0, rows) + own(m2, x, r0, rows)
        total = total + own(n0, x, r0, rows) + v + value
        put(gm, x, r0, rows, coefficient(1) * total + own(bm, x + 1, r0, rows))
    sweep(10, n1, medium_total, 11, gm)
    arrive_all(11, gm)
    prolong(gm, bf)
    arrive_all(12, g3)
    correct(bf, g3, h0, 1.0)
    sweep(None, h0, smooth_to(h1), 13, h1)

    def first_terms(x, r0, rows):
        total = own(f0, x, r0, rows) + own(f1, x, r0, rows) + own(f2, x, r0, rows)
        total = total + own(h0, x, r0, rows)
        rhs[x - 1, pl.ds(r0, rows), :] = coefficient(0) * total + own(bf, x + 1, r0, rows)
    plane_op(h0, 1, NX, first_terms)

    def last_terms(x, r0, rows, v, nb):
        value = (1.0 - W) * v + (W / 6.0) * nb
        before = rhs[x - 1, pl.ds(r0, rows), :]
        rhs[x - 1, pl.ds(r0, rows), :] = before + coefficient(0) * (v + value)
    sweep(13, h1, last_terms, edge_first=scatter, between=gather)
    finish_faces()
    for rnd, buf in sent.items():
        for d in sides(buf):
            @pl.when(has[d])
            def _():
                for c in range(chunks(buf, d)):
                    copy(rnd, buf, d, c).wait_send()


def run_cycle(cotangent, seg_rows, owners, offsets):
    S, Q = lax.axis_size("slab"), lax.axis_size("pencil")
    x, y, z = cotangent.shape
    pieces = min(S, y // EDGE)
    R = y // pieces
    targets = source_rows(seg_rows, owners, offsets, TILE)
    first = jnp.minimum(lax.axis_index("slab"), pieces - 1) * R
    goal = lax.dynamic_slice_in_dim(targets, first, R, axis=1).reshape(1, -1)

    def padded(level, deep=1):
        k = 2**level
        return pltpu.VMEM((x // k + 2 * deep, y // k + 2 * EDGE, z // k), jnp.float32)
    scratch = [padded(0)] * 4 + [padded(1)] * 4 + [padded(2)] * 3
    scratch += [padded(1, 2)] + [padded(1)] * 3 + [padded(0, 2)] + [padded(0)] * 2
    scratch += [
        pltpu.VMEM((2, Q, R, z), jnp.float32),
        pltpu.VMEM((goal.shape[1], TILE), jnp.float32),
        pltpu.VMEM((S, TILE, TILE), jnp.float32),
        pltpu.VMEM((S, TILE, TILE), jnp.float32),
        pltpu.VMEM((S * TILE, goal.shape[1]), jnp.bfloat16),
        pltpu.SemaphoreType.DMA,
        pltpu.SemaphoreType.DMA((ROUNDS, 8, CHUNKS)),
        pltpu.SemaphoreType.DMA((ROUNDS, 8, CHUNKS)),
        pltpu.SemaphoreType.DMA((2, pieces)),
        pltpu.SemaphoreType.DMA((2,)),
        pltpu.SemaphoreType.DMA((Q,)),
        pltpu.SemaphoreType.DMA((Q,)),
        pltpu.SemaphoreType.DMA((S,)),
        pltpu.SemaphoreType.DMA((S,)),
    ]
    return pl.pallas_call(
        functools.partial(cycle_kernel, S, Q, pieces),
        out_shape=(
            jax.ShapeDtypeStruct(cotangent.shape, jnp.float32),
            jax.ShapeDtypeStruct((1, TILE, TILE), jnp.float32),
        ),
        in_specs=[pl.BlockSpec(memory_space=pl.ANY), pl.BlockSpec(memory_space=pltpu.VMEM)],
        out_specs=(pl.BlockSpec(memory_space=pltpu.VMEM), pl.BlockSpec(memory_space=pltpu.VMEM)),
        scratch_shapes=scratch,
        compiler_params=pltpu.CompilerParams(
            collective_id=0, has_side_effects=True, vmem_limit_bytes=48 * 2**20
        ),
        name="vcycle",
    )(cotangent, goal)


def source_rows(seg_rows, owners, offsets, tile_size):
    starts = jnp.cumsum(seg_rows, axis=1) - seg_rows
    position = jnp.arange(tile_size, dtype=jnp.int32)[None, None, :]
    inside = (position >= starts[:, :, None]) & (position < (starts + seg_rows)[:, :, None])
    value = owners[:, :, None] * tile_size + offsets[:, :, None] + position - starts[:, :, None]
    return jnp.sum(jnp.where(inside, value, 0), axis=1)


def shards(cotangent, seg_rows, owners, offsets):
    rhs_grad, parent_grad = run_cycle(cotangent, seg_rows, owners, offsets)
    return (rhs_grad, parent_grad)


def solution(mesh):
    return jax.shard_map(
        shards,
        mesh=mesh,
        in_specs=(P("slab", "pencil", None), P(), P(), P()),
        out_specs=(P("slab", "pencil", None), P(("slab", "pencil"), None, None)),
        check_vma=False,
    )
```
